512 devices in a mesh: orb: 16 (over z, core), box: 32 (over y, x).
Axes of the slice: x: 4, y: 8, z: 8, core: 2. Of those that a mesh axis runs over, the one named last changes fastest.
Arguments:
- coarse: bfloat16 [16, 8, 729, 4096], P('orb', None, None, 'box'), may hold values from -1.5 to 1.5
- wavelets: bfloat16 [16, 7, 729, 4096], P('orb', None, None, 'box'), may hold values from -1.5 to 1.5
- leaf_flags: int32 [16, 4096], P('orb', 'box'), may hold values 0 or 1
- child_key1: int32 [4096], P('box'), may hold values from 0 to 32767, as said below
- child_key2: int32 [8192], P('box'), may hold values from 0 to 32767, as said below
- counts: int32 [32], P('box'), may hold values from 128 to 256, as said below
Outputs:
- density: float32 [729, 8192], P(None, 'box')
The draws below stay inside these ranges and needn't reach their ends.
Inputs may be any that keep to these rules, and one draw needn't show every extreme that they name: `child_key1`: within each curve range of 128 entries the keys rise and name distinct children; each parent lies in the same range or among the last 32 boxes of the range before; every range but the first has an entry naming a child of the first of those 32 boxes. `child_key2`: within each curve range of 256 entries the keys rise and name distinct children; each parent lies in the same range or among the last 32 boxes of the range before; every range but the first has an entry naming a child of the first of those 32 boxes. `counts`: some range is full in every draw and some range holds the fewest.
All inputs are finite; a program needn't handle non-finite values. No bound on the sum of `leaf_flags` on one device may be relied on, other than what follows from the above.
Results may differ from the reference program's by a relative error of at most 0.0003.
Values may be sent and summed in bfloat16 or wider, within the bound.
No kernel may reach another device: no remote copies, remote signals or barrier semaphores. Data moves between devices by JAX's collectives and lax.ppermute only.
A program may use at most 64 MiB of HBM per device.

```python
import math
import jax
import jax.numpy as jnp
import numpy as np
from jax import lax

BOX_DEV = 128
ORBITALS = 16
BOXES = 4096
LEAVES = 8192
SPILL = 32


def range_keys(key, slots):
    ranges = BOXES // BOX_DEV
    margin = 8 * SPILL
    choices_all = 8 * (BOX_DEV + SPILL)
    choices_first = 8 * BOX_DEV

    def one_range(position):
        folded = jax.random.fold_in(key, position)
        key_rest, key_first = jax.random.split(folded)
        middle = 1 + jax.random.permutation(key_rest, choices_all - 2)[:slots - 2]
        picked = jnp.concatenate([jnp.zeros((1,), jnp.int32), middle.astype(jnp.int32), jnp.full((1,), choices_all - 1, jnp.int32)])
        earlier = picked < margin
        shifted = picked - margin
        parent = jnp.where(earlier, (position - 1) * BOX_DEV + BOX_DEV - SPILL + picked // 8, position * BOX_DEV + shifted // 8)
        octant = jnp.where(earlier, picked % 8, shifted % 8)
        general = 8 * parent + octant
        middle_first = 1 + jax.random.permutation(key_first, choices_first - 2)[:slots - 2]
        first_codes = jnp.concatenate([jnp.zeros((1,), jnp.int32), middle_first.astype(jnp.int32), jnp.full((1,), choices_first - 1, jnp.int32)])
        codes = jnp.where(position == 0, first_codes, general)
        return jnp.sort(codes)
    return jax.vmap(one_range)(jnp.arange(ranges, dtype=jnp.int32)).reshape(-1).astype(jnp.int32)


def draw_child_key1(key, part):
    return range_keys(jax.random.fold_in(key, 11), BOX_DEV)


def draw_child_key2(key, part):
    return range_keys(jax.random.fold_in(key, 23), 2 * BOX_DEV)


def draw_counts(key, part):
    ranges = BOXES // BOX_DEV
    key_all, key_full, key_low = jax.random.split(jax.random.fold_in(key, 37), 3)
    values = jax.random.randint(key_all, (ranges,), BOX_DEV, 2 * BOX_DEV + 1, dtype=jnp.int32)
    fullest = jax.random.randint(key_full, (), 0, ranges, dtype=jnp.int32)
    lowest = (fullest + 1 + jax.random.randint(key_low, (), 0, ranges - 1, dtype=jnp.int32)) % ranges
    positions = jnp.arange(ranges, dtype=jnp.int32)
    values = jnp.where(positions == fullest, 2 * BOX_DEV, values)
    values = jnp.where(positions == lowest, BOX_DEV, values)
    return values.astype(jnp.int32)


def place_ends(values, stream_key, least, top_value):
    index_at = [jax.random.randint(jax.random.fold_in(stream_key, axis), (), 0, length) for axis, length in enumerate(values.shape)]
    widest = values.shape.index(max(values.shape))
    next_to = index_at[:widest] + [(index_at[widest] + 1) % values.shape[widest]] + index_at[widest + 1:]
    return values.at[tuple(index_at)].set(least).at[tuple(next_to)].set(top_value)


def levels(rng, shape, pieces, low, largest):
    loudness, own = 1.0, jax.random.fold_in(rng, 6)
    for dim, parts in pieces:
        draws = jnp.exp(jax.random.uniform(jax.random.fold_in(own, dim), (parts,), jnp.float32, low / len(pieces), largest / len(pieces)))
        loudness = loudness * jnp.repeat(draws, shape[dim] // parts).reshape([-1 if axis == dim else 1 for axis in range(len(shape))])
    return loudness


def normal_values(key, dims, scale, reach, pieces=(), kind=jnp.bfloat16):
    values = jax.random.normal(key, dims, jnp.float32) * scale
    if len(pieces) > 0:
        values = levels(key, dims, pieces, -0.22, 0.18) * values
    return jnp.clip(values, min=-reach, max=reach).astype(kind)


def setup_inputs(seed: int = 0) -> dict:
    splits = jax.random.split(jax.random.key(seed), 7)
    return {
        "coarse": normal_values(splits[0], (ORBITALS, 8, 729, BOXES), 0.25, 1.5, ((0, 16), (3, 32))),
        "wavelets": normal_values(splits[1], (ORBITALS, 7, 729, BOXES), 0.25, 1.5, ((0, 16), (3, 32))),
        "leaf_flags": place_ends((jax.random.randint(splits[2], (ORBITALS, BOXES), 0, 2) < 1).astype(jnp.int32), jax.random.fold_in(splits[2], 1), 0, 1),
        "child_key1": draw_child_key1(jax.random.fold_in(splits[6], 71), 0),
        "child_key2": draw_child_key2(jax.random.fold_in(splits[6], 71), 0),
        "counts": draw_counts(jax.random.fold_in(splits[6], 71), 0),
    }


def legendre_pair(order, where):
    before = where * 0.0 + 1.0
    value = where
    for degree in range(1, order):
        before, value = (value, ((2 * degree + 1) * where * value - degree * before) / (degree + 1))
    return (value, before)

def gauss_rule(order):
    nodes = np.cos(np.pi * (np.arange(order) + 0.75) / (order + 0.5))
    for repeat in range(40):
        value, before = legendre_pair(order, nodes)
        slope = order * (nodes * value - before) / (nodes * nodes - 1.0)
        nodes = nodes - value / slope
    value, before = legendre_pair(order, nodes)
    slope = order * (nodes * value - before) / (nodes * nodes - 1.0)
    weights = 2.0 / ((1.0 - nodes * nodes) * slope * slope)
    return (nodes[::-1], weights[::-1])

def legendre_basis(where):
    shifted = 2.0 * where - 1.0
    rows = [shifted * 0.0 + 1.0, shifted]
    for degree in range(1, 8):
        rows.append(((2 * degree + 1) * shifted * rows[degree] - degree * rows[degree - 1]) / (degree + 1))
    scale = np.sqrt(2.0 * np.arange(9) + 1.0)[:, None]
    return np.stack(rows, 0) * scale

def complement_rows(scaling_rows):
    members = [scaling_rows[index] for index in range(9)]
    kept = []
    identity = np.eye(18)
    for column in range(18):
        vector = identity[column]
        for passes in range(2):
            for member in members + kept:
                vector = vector - np.dot(member, vector) * member
        length = np.sqrt(np.dot(vector, vector))
        if length > 0.1 and len(kept) < 9:
            kept.append(vector / length)
    return np.stack(kept, 0)

def wavelet_tables():
    nodes, weights = gauss_rule(24)
    points = 0.5 * (nodes + 1.0)
    halves = 0.5 * weights
    lower = legendre_basis(0.5 * points) * halves @ legendre_basis(points).T / math.sqrt(2.0)
    upper = legendre_basis(0.5 * points + 0.5) * halves @ legendre_basis(points).T / math.sqrt(2.0)
    scaling_rows = np.concatenate([lower, upper], 1)
    wavelet_rows = complement_rows(scaling_rows)
    matrix = np.concatenate([scaling_rows, wavelet_rows], 0).reshape(2, 9, 2, 9)
    gauss, gauss_weights = gauss_rule(9)
    quad = legendre_basis(0.5 * (gauss + 1.0)).T * np.sqrt(0.5 * gauss_weights)[:, None]
    return (jnp.asarray(matrix, dtype=jnp.float32), jnp.asarray(quad, dtype=jnp.float32))

def expand(blocks, filters):
    highest = lax.Precision.HIGHEST
    cube = blocks.reshape(2, 2, 2, 9, 9, 9, -1)
    cube = jnp.einsum('abcijlz,aiod->bcjlodz', cube, filters, precision=highest)
    cube = jnp.einsum('bcjlodz,bjqe->clodqez', cube, filters, precision=highest)
    cube = jnp.einsum('clodqez,clrf->defoqrz', cube, filters, precision=highest)
    return cube.reshape(729, 8, -1)

def select(children, codes):
    width = children.shape[2]
    flat = children.reshape(729, 8 * width)
    index = (codes % 8 * width + codes // 8).astype(jnp.int32)
    return jnp.take(flat, index, axis=1)

def quadrature(scaling, quad):
    highest = lax.Precision.HIGHEST
    cube = scaling.reshape(9, 9, 9, -1)
    cube = jnp.einsum('ijlz,gi->gjlz', cube, quad, precision=highest)
    cube = jnp.einsum('gjlz,hj->ghlz', cube, quad, precision=highest)
    cube = jnp.einsum('ghlz,kl->ghkz', cube, quad, precision=highest)
    return cube.reshape(729, -1)

def reference(coarse, wavelets, leaf_flags, child_key1, child_key2, counts):
    filters, quad = wavelet_tables()

    def orbital_step(total, items):
        coarse_one, wave_one, leaf_one = items
        children = expand(coarse_one.astype(jnp.float32), filters)
        first = select(children, child_key1)
        keep = (1 - leaf_one).astype(jnp.float32)
        blocks = jnp.concatenate([first[None], wave_one.astype(jnp.float32) * keep], 0)
        children = expand(blocks, filters)
        second = select(children, child_key2)
        values = quadrature(second, quad)
        return (total + values * values, None)
    start = jnp.zeros((729, LEAVES), jnp.float32)
    total, unused = lax.scan(orbital_step, start, (coarse, wavelets, leaf_flags))
    slots = jnp.arange(LEAVES, dtype=jnp.int32)
    live = slots % (2 * BOX_DEV) < counts[slots // (2 * BOX_DEV)]
    return 2.0 * total * live.astype(jnp.float32)
```

```python
import functools
import math

import jax
import jax.numpy as jnp
import numpy as np
from jax import lax
from jax.experimental import pallas as pl
from jax.experimental.pallas import tpu as pltpu
from jax.sharding import PartitionSpec as P

BOX_DEV = 128
SPILL = 32
SLOTS = 256
LANES = 128
PLANE = 88
WINDOW = 96
CHUNKS = 16
CHUNK = 48
HELD = 46
STEPS = (64, 32, 16, 8, 8, 4, 2, 1)
VMEM_BYTES = 48 * 1024 * 1024


def shifted_2(value, axis, steps):
    count = lax.axis_size(axis)
    first, last = (max(0, -steps), min(count, count - steps))
    return lax.ppermute(value, axis, [(source, source + steps) for source in range(first, last)])


def legendre_pair(order, where):
    before = where * 0.0 + 1.0
    value = where
    for degree in range(1, order):
        before, value = (value, ((2 * degree + 1) * where * value - degree * before) / (degree + 1))
    return (value, before)


def gauss_rule(order):
    nodes = np.cos(np.pi * (np.arange(order) + 0.75) / (order + 0.5))
    for repeat in range(40):
        value, before = legendre_pair(order, nodes)
        slope = order * (nodes * value - before) / (nodes * nodes - 1.0)
        nodes = nodes - value / slope
    value, before = legendre_pair(order, nodes)
    slope = order * (nodes * value - before) / (nodes * nodes - 1.0)
    weights = 2.0 / ((1.0 - nodes * nodes) * slope * slope)
    return (nodes[::-1], weights[::-1])


def legendre_basis(where):
    shifted = 2.0 * where - 1.0
    rows = [shifted * 0.0 + 1.0, shifted]
    for degree in range(1, 8):
        rows.append(
            ((2 * degree + 1) * shifted * rows[degree] - degree * rows[degree - 1]) / (degree + 1)
        )
    scale = np.sqrt(2.0 * np.arange(9) + 1.0)[:, None]
    return np.stack(rows, 0) * scale


def complement_rows(scaling_rows):
    members = [scaling_rows[index] for index in range(9)]
    kept = []
    identity = np.eye(18)
    for column in range(18):
        vector = identity[column]
        for passes in range(2):
            for member in members + kept:
                vector = vector - np.dot(member, vector) * member
        length = np.sqrt(np.dot(vector, vector))
        if length > 0.1 and len(kept) < 9:
            kept.append(vector / length)
    return np.stack(kept, 0)


def wavelet_tables():
    nodes, weights = gauss_rule(24)
    points = 0.5 * (nodes + 1.0)
    halves = 0.5 * weights
    lower = legendre_basis(0.5 * points) * halves @ legendre_basis(points).T / math.sqrt(2.0)
    upper = legendre_basis(0.5 * points + 0.5) * halves @ legendre_basis(points).T / math.sqrt(2.0)
    scaling_rows = np.concatenate([lower, upper], 1)
    wavelet_rows = complement_rows(scaling_rows)
    matrix = np.concatenate([scaling_rows, wavelet_rows], 0).reshape(2, 9, 2, 9)
    gauss, gauss_weights = gauss_rule(9)
    quad = legendre_basis(0.5 * (gauss + 1.0)).T * np.sqrt(0.5 * gauss_weights)[:, None]
    return (matrix, quad)


def bf16_pair(table):
    high = table.astype(np.float32).astype(jnp.bfloat16)
    low = (table - high.astype(np.float64)).astype(np.float32).astype(jnp.bfloat16)
    return (high, low)


def plane_filters(matrix, blocks):
    plane = np.einsum("bjqe,clrf->qrefbcjl", matrix, matrix).reshape(4, 81, 4, 81)[:, :, :blocks]
    tables = np.zeros((9, 4, PLANE, blocks, WINDOW))
    for index in range(9):
        tables[index, :, :81, :, index : index + 81] = plane
    return bf16_pair(tables.reshape(9, 4 * PLANE, blocks * WINDOW))


def line_filters(matrix):
    table = matrix.reshape(18, 2, 9).transpose(1, 0, 2).reshape(2, 162)
    return np.broadcast_to(table[:, :, None], (2, 162, LANES)).astype(np.float32)


def tables():
    matrix, quad = wavelet_tables()
    rows = matrix.reshape(2, 9, 2, 9)
    points = np.einsum("aiop,gp->aiog", rows, quad)
    result = {"line1": line_filters(rows), "line2": line_filters(points)}
    for name, filters in (("plane1", rows), ("plane2", points)):
        high, low = plane_filters(filters, 4)
        result[name] = np.concatenate([high, low], 2)
    high, low = plane_filters(points, 1)
    result["plane3"] = np.concatenate([high, high, low], 2)
    return result


def dot(left, right):
    return jnp.dot(left, right, preferred_element_type=jnp.float32)


def spill_selectors():
    row = lax.broadcasted_iota(jnp.int32, (LANES, LANES), 0)
    column = lax.broadcasted_iota(jnp.int32, (LANES, LANES), 1)
    return [
        jnp.where((row - (BOX_DEV - SPILL) == column - SPILL * k) & (row >= BOX_DEV - SPILL), 1.0, 0.0).astype(
            jnp.bfloat16
        )
        for k in range(4)
    ]


def parent_selectors(relative):
    slots = relative.shape[1]
    parent = relative >> 3
    row = lax.broadcasted_iota(jnp.int32, (2 * LANES, slots), 0)
    return [
        jnp.where(row == jnp.where(parent >= 0, parent, parent + BOX_DEV + SPILL * (k + 1)), 1.0, 0.0).astype(
            jnp.bfloat16
        )
        for k in range(4)
    ]


def pack_coarse_kernel(coarse_ref, out_ref):
    selectors = spill_selectors()
    for group in range(2):
        total = dot(coarse_ref[0, 4 * group], selectors[0])
        for k in range(1, 4):
            total += dot(coarse_ref[0, 4 * group + k], selectors[k])
        out_ref[group] = total.astype(jnp.bfloat16)


def pack_wavelets_kernel(wavelet_ref, leaf_ref, out_ref):
    keep = (1 - leaf_ref[...]).astype(jnp.float32)
    selectors = spill_selectors()
    for group in range(2):
        total = None
        for k in range(4):
            block = 4 * group + k
            if block > 0:
                term = dot((wavelet_ref[0, block - 1].astype(jnp.float32) * keep).astype(jnp.bfloat16), selectors[k])
                total = term if total is None else total + term
        out_ref[group] = total.astype(jnp.bfloat16)


def gather_block(block, halo, selector, wide_ref, target_ref, index):
    wide_ref[0:729] = dot(jnp.concatenate([block, halo], axis=1), selector)
    target_ref[index] = wide_ref[...].astype(jnp.bfloat16)


def choose_plane(planes, octant):
    upper, right = ((octant >> 1) & 1) == 1, (octant & 1) == 1
    parts = [planes[PLANE * k : PLANE * (k + 1)] for k in range(4)]
    return jnp.where(upper, jnp.where(right, parts[3], parts[2]), jnp.where(right, parts[1], parts[0]))


def line_coefficients(octant, line_ref, coef_ref):
    slots = octant.shape[1]
    for part in range(slots // LANES):
        lanes = slice(LANES * part, LANES * (part + 1))
        coef_ref[0:162, lanes] = jnp.where((octant[:, lanes] >> 2) == 1, line_ref[1], line_ref[0])


def planes_of_blocks(gathered_ref, plane_ref, octant, chosen_ref):
    slots = octant.shape[1]
    both = jnp.concatenate([octant, octant], axis=1)
    for i in range(9):
        rows = slice(80 * i, 80 * i + WINDOW)
        halves = [jnp.concatenate([gathered_ref[4 * a + k, rows] for k in range(4)], axis=0) for a in range(2)]
        data = jnp.concatenate(halves, axis=1)
        planes = dot(plane_ref[i], jnp.concatenate([data, data], axis=0))
        chosen = choose_plane(planes, both)
        chosen_ref[i] = chosen[:, :slots]
        chosen_ref[9 + i] = chosen[:, slots:]


def line_sum(p, count, coef_ref, chosen_ref, start):
    total = start
    for index in range(count):
        row = index * 9 + p
        term = coef_ref[row : row + 1] * chosen_ref[index]
        total = term if total is None else total + term
    return total


def level1_kernel(coarse_ref, halo_ref, relative_ref, plane_ref, line_ref, pair_ref, spill_ref, gathered_ref, wide_ref, chosen_ref, coef_ref, box_ref):
    relative = relative_ref[...]
    octant = relative & 7
    selectors = parent_selectors(relative)
    wide_ref[728:736] = jnp.zeros((8, BOX_DEV), jnp.float32)
    for block in range(8):
        gather_block(coarse_ref[0, block], halo_ref[block // 4], selectors[block % 4], wide_ref, gathered_ref, block)
    line_coefficients(octant, line_ref, coef_ref)
    planes_of_blocks(gathered_ref, plane_ref, octant, chosen_ref)
    box_ref[728:768] = jnp.zeros((40, BOX_DEV), jnp.float32)
    for p in range(9):
        box_ref[81 * p : 81 * p + PLANE] = line_sum(p, 18, coef_ref, chosen_ref, None)
    scaling = box_ref[...]
    high = scaling.astype(jnp.bfloat16)
    low = (scaling - high.astype(jnp.float32)).astype(jnp.bfloat16)
    spill = spill_selectors()
    for index, part in enumerate((high, low)):
        pair_ref[index] = part
        total = dot(part[0:192], spill[0])
        for k in range(1, 4):
            total += dot(part[192 * k : 192 * (k + 1)], spill[k])
        spill_ref[index] = total.astype(jnp.bfloat16)


def wavelet_kernel(wavelet_ref, halo_ref, leaf_ref, relative_ref, plane_ref, line_ref, after_ref, out_ref, gathered_ref, wide_ref, chosen_ref, coef_ref):
    relative = relative_ref[...]
    octant = relative & 7
    keep = (1 - leaf_ref[...]).astype(jnp.float32)
    selectors = parent_selectors(relative)
    wide_ref[728:736] = jnp.zeros((8, SLOTS), jnp.float32)
    gathered_ref[0] = jnp.zeros((736, SLOTS), jnp.bfloat16)
    for block in range(1, 8):
        own = (wavelet_ref[0, block - 1].astype(jnp.float32) * keep).astype(jnp.bfloat16)
        gather_block(own, halo_ref[block // 4], selectors[block % 4], wide_ref, gathered_ref, block)
    line_coefficients(octant, line_ref, coef_ref)
    planes_of_blocks(gathered_ref, plane_ref, octant, chosen_ref)
    for p in range(9):
        out_ref[p] = line_sum(p, 18, coef_ref, chosen_ref, None)


def encode(values, code_ref, targets, largest_ref, scale_ref, power_ref):
    row = lax.broadcasted_iota(jnp.int32, (CHUNK, SLOTS), 0)
    for index, value in enumerate(values):
        largest_ref[index : index + 1] = jnp.max(jnp.where(row < HELD, value(), 0.0), axis=0, keepdims=True)
    largest = largest_ref[...]
    scale = jnp.full(largest.shape, 2.0**-16, jnp.float32)
    power = jnp.zeros(largest.shape, jnp.int32)
    for step in STEPS:
        longer = scale * 2.0**step
        fits = largest * longer < 32766.0
        scale = jnp.where(fits, longer, scale)
        power = jnp.where(fits, power + step, power)
    scale_ref[...] = scale
    power_ref[...] = power
    for index, value in enumerate(values):
        code = jnp.round(value() * scale_ref[index : index + 1]).astype(jnp.int32)
        code = jnp.where(row < HELD, code, power_ref[index : index + 1]).astype(jnp.int16)
        for target in targets(index):
            code_ref[target] = code


def decode_scales(code_ref, power_ref):
    for index in range(CHUNKS):
        tail = code_ref[index, CHUNK - 16 : CHUNK].astype(jnp.int32)
        power_ref[index : index + 1] = tail[15:16]
    power = power_ref[...]
    scale = jnp.full(power.shape, 2.0**16, jnp.float32)
    for step in STEPS:
        taken = power >= step
        scale = jnp.where(taken, scale * 2.0**-step, scale)
        power = jnp.where(taken, power - step, power)
    return scale


def density_kernel(pair_ref, halo_ref, relative_ref, count_ref, plane_ref, line_ref, before_ref, code_ref, gathered_ref, chosen_ref, coef_ref, dense_ref, largest_ref, scale_ref, power_ref):
    relative = relative_ref[...]
    octant = relative & 7
    selectors = parent_selectors(relative)
    for index in range(2):
        for k in range(4):
            rows = slice(192 * k, 192 * (k + 1))
            both = jnp.concatenate([pair_ref[index, rows], halo_ref[index]], axis=1)
            gathered_ref[index, rows] = dot(both, selectors[k]).astype(jnp.bfloat16)
    line_coefficients(octant, line_ref, coef_ref)
    for i in range(9):
        rows = slice(80 * i, 80 * i + WINDOW)
        high = gathered_ref[0, rows]
        planes = dot(plane_ref[i], jnp.concatenate([high, gathered_ref[1, rows], high], axis=0))
        chosen_ref[i] = choose_plane(planes, octant)
    slot = lax.broadcasted_iota(jnp.int32, (1, SLOTS), 1)
    factor = jnp.where(slot < count_ref[0, 0], 2.0, 0.0)
    dense_ref[728:744] = jnp.zeros((16, SLOTS), jnp.float32)
    for p in range(9):
        value = line_sum(p, 9, coef_ref, chosen_ref, before_ref[p])
        dense_ref[81 * p : 81 * p + PLANE] = value * value * factor
    chunks = [lambda c=c: dense_ref[HELD * c : HELD * c + CHUNK] for c in range(CHUNKS)]
    encode(chunks, code_ref, lambda index: (index,), largest_ref, scale_ref, power_ref)


def add_kernel(code_ref, out_ref, power_ref, inverse_ref, total_ref, largest_ref, scale_ref, shared_ref):
    inverse_ref[...] = decode_scales(code_ref, power_ref)
    total = None
    for index in range(CHUNKS):
        term = code_ref[index].astype(jnp.int32).astype(jnp.float32) * inverse_ref[index : index + 1]
        total = term if total is None else total + term
    total_ref[...] = total
    encode([lambda: total_ref[...]], out_ref, lambda index: range(CHUNKS), largest_ref, scale_ref, shared_ref)


def finish_kernel(code_ref, out_ref, power_ref, inverse_ref):
    inverse_ref[...] = decode_scales(code_ref, power_ref)
    for index in range(CHUNKS):
        rows = min(HELD, 729 - HELD * index)
        value = code_ref[index].astype(jnp.int32).astype(jnp.float32) * inverse_ref[index : index + 1]
        out_ref[HELD * index : HELD * index + rows] = value[0:rows]


def call(kernel, outs, scratch, *operands, scalar=()):
    spaces = [pltpu.SMEM if index in scalar else pltpu.VMEM for index in range(len(operands))]
    return pl.pallas_call(
        kernel,
        out_shape=outs,
        in_specs=[pl.BlockSpec(memory_space=space) for space in spaces],
        out_specs=jax.tree.map(lambda out: pl.BlockSpec(memory_space=pltpu.VMEM), outs),
        scratch_shapes=[pltpu.VMEM(shape, kind) for shape, kind in scratch],
        compiler_params=pltpu.CompilerParams(vmem_limit_bytes=VMEM_BYTES),
    )(*operands)


def struct(shape, kind):
    return jax.ShapeDtypeStruct(shape, kind)


def level1(coarse, halo, relative1, table):
    return call(
        level1_kernel,
        [struct((2, 768, BOX_DEV), jnp.bfloat16), struct((2, 192, LANES), jnp.bfloat16)],
        [
            ((8, 736, BOX_DEV), jnp.bfloat16),
            ((736, BOX_DEV), jnp.float32),
            ((18, PLANE, BOX_DEV), jnp.float32),
            ((168, BOX_DEV), jnp.float32),
            ((768, BOX_DEV), jnp.float32),
        ],
        coarse, halo, relative1, table["plane1"], table["line1"],
    )


def wavelet_part(wavelets, halo, leaf_flags, relative2, table, after):
    return call(
        wavelet_kernel,
        struct((9, PLANE, SLOTS), jnp.float32),
        [
            ((8, 736, SLOTS), jnp.bfloat16),
            ((736, SLOTS), jnp.float32),
            ((18, PLANE, SLOTS), jnp.float32),
            ((168, SLOTS), jnp.float32),
        ],
        wavelets, halo, leaf_flags, relative2, table["plane2"], table["line2"], after,
    )


def density_codes(pair, halo, relative2, counts, table, before):
    return call(
        density_kernel,
        struct((CHUNKS, CHUNK, SLOTS), jnp.int16),
        [
            ((2, 768, SLOTS), jnp.bfloat16),
            ((9, PLANE, SLOTS), jnp.float32),
            ((168, SLOTS), jnp.float32),
            ((744, SLOTS), jnp.float32),
            ((CHUNKS, SLOTS), jnp.float32),
            ((CHUNKS, SLOTS), jnp.float32),
            ((CHUNKS, SLOTS), jnp.int32),
        ],
        pair, halo, relative2, counts, table["plane3"], table["line2"], before, scalar=(3,),
    )


def add_codes(codes):
    return call(
        add_kernel,
        struct((CHUNKS, CHUNK, SLOTS), jnp.int16),
        [
            ((CHUNKS, SLOTS), jnp.int32),
            ((CHUNKS, SLOTS), jnp.float32),
            ((CHUNK, SLOTS), jnp.float32),
            ((1, SLOTS), jnp.float32),
            ((1, SLOTS), jnp.float32),
            ((1, SLOTS), jnp.int32),
        ],
        codes,
    )


def finish(codes):
    return call(
        finish_kernel,
        struct((729, SLOTS), jnp.float32),
        [((CHUNKS, SLOTS), jnp.int32), ((CHUNKS, SLOTS), jnp.float32)],
        codes,
    )


def shards(table, coarse, wavelets, leaf_flags, child_key1, child_key2, counts):
    position = lax.axis_index("box")
    relative1 = (child_key1 - position * (8 * BOX_DEV)).reshape(1, BOX_DEV)
    relative2 = (child_key2 - position * (8 * BOX_DEV)).reshape(1, SLOTS)
    packed = call(pack_coarse_kernel, struct((2, 729, LANES), jnp.bfloat16), [], coarse)
    coarse_halo = shifted_2(packed, "box", 1)
    packed = call(pack_wavelets_kernel, struct((2, 729, LANES), jnp.bfloat16), [], wavelets, leaf_flags)
    wavelet_halo = shifted_2(packed, "box", 1)
    pair, spill = level1(coarse, coarse_halo, relative1, table)
    pair_halo = shifted_2(spill, "box", 1)
    before = wavelet_part(wavelets, wavelet_halo, leaf_flags, relative2, table, spill)
    codes = density_codes(pair, pair_halo, relative2, counts.reshape(1, 1), table, before)
    codes = lax.all_to_all(codes, "orb", 0, 0, tiled=True)
    codes = lax.all_to_all(add_codes(codes), "orb", 0, 0, tiled=True)
    return finish(codes)


def solution(mesh):
    in_specs = (
        P("orb", None, None, "box"),
        P("orb", None, None, "box"),
        P("orb", "box"),
        P("box"),
        P("box"),
        P("box"),
    )
    out_specs = P(None, "box")
    table = {name: jnp.asarray(value) for name, value in tables().items()}
    local = functools.partial(shards, table)
    return jax.shard_map(local, mesh=mesh, in_specs=in_specs, out_specs=out_specs, check_vma=False)
```

```python
import functools
import math

import jax
import jax.numpy as jnp
import numpy as np
from jax import lax
from jax.experimental import pallas as pl
from jax.experimental.pallas import tpu as pltpu
from jax.sharding import PartitionSpec as P

BOX_DEV = 128
SPILL = 32
SLOTS = 256
LANES = 128
PLANE = 88
WINDOW = 96
ROWS = 8 * 729
PART = 1472
TALL = 744
CHUNKS = 16
CHUNK = 48
HELD = 46
STEPS = (64, 32, 16, 8, 8, 4, 2, 1)
VMEM_BYTES = 20 * 1024 * 1024


def shifted_2(value, axis, steps):
    count = lax.axis_size(axis)
    first, last = (max(0, -steps), min(count, count - steps))
    return lax.ppermute(value, axis, [(source, source + steps) for source in range(first, last)])


def legendre_pair(order, where):
    before = where * 0.0 + 1.0
    value = where
    for degree in range(1, order):
        before, value = (value, ((2 * degree + 1) * where * value - degree * before) / (degree + 1))
    return (value, before)


def gauss_rule(order):
    nodes = np.cos(np.pi * (np.arange(order) + 0.75) / (order + 0.5))
    for repeat in range(40):
        value, before = legendre_pair(order, nodes)
        slope = order * (nodes * value - before) / (nodes * nodes - 1.0)
        nodes = nodes - value / slope
    value, before = legendre_pair(order, nodes)
    slope = order * (nodes * value - before) / (nodes * nodes - 1.0)
    weights = 2.0 / ((1.0 - nodes * nodes) * slope * slope)
    return (nodes[::-1], weights[::-1])


def legendre_basis(where):
    shifted = 2.0 * where - 1.0
    rows = [shifted * 0.0 + 1.0, shifted]
    for degree in range(1, 8):
        rows.append(
            ((2 * degree + 1) * shifted * rows[degree] - degree * rows[degree - 1]) / (degree + 1)
        )
    scale = np.sqrt(2.0 * np.arange(9) + 1.0)[:, None]
    return np.stack(rows, 0) * scale


def complement_rows(scaling_rows):
    members = [scaling_rows[index] for index in range(9)]
    kept = []
    identity = np.eye(18)
    for column in range(18):
        vector = identity[column]
        for passes in range(2):
            for member in members + kept:
                vector = vector - np.dot(member, vector) * member
        length = np.sqrt(np.dot(vector, vector))
        if length > 0.1 and len(kept) < 9:
            kept.append(vector / length)
    return np.stack(kept, 0)


def wavelet_tables():
    nodes, weights = gauss_rule(24)
    points = 0.5 * (nodes + 1.0)
    halves = 0.5 * weights
    lower = legendre_basis(0.5 * points) * halves @ legendre_basis(points).T / math.sqrt(2.0)
    upper = legendre_basis(0.5 * points + 0.5) * halves @ legendre_basis(points).T / math.sqrt(2.0)
    scaling_rows = np.concatenate([lower, upper], 1)
    wavelet_rows = complement_rows(scaling_rows)
    matrix = np.concatenate([scaling_rows, wavelet_rows], 0).reshape(2, 9, 2, 9)
    gauss, gauss_weights = gauss_rule(9)
    quad = legendre_basis(0.5 * (gauss + 1.0)).T * np.sqrt(0.5 * gauss_weights)[:, None]
    return (matrix, quad)


def bf16_pair(table):
    high = table.astype(np.float32).astype(jnp.bfloat16)
    low = (table - high.astype(np.float64)).astype(np.float32).astype(jnp.bfloat16)
    return (high, low)


def plane_filters(matrix, blocks, shifts):
    plane = np.einsum("bjqe,clrf->qrefbcjl", matrix, matrix).reshape(4, 81, 4, 81)[:, :, :blocks]
    tables = np.zeros((shifts, 4, PLANE, blocks, WINDOW))
    for index in range(shifts):
        tables[index, :, :81, :, index : index + 81] = plane
    return bf16_pair(tables.reshape(shifts, 4 * PLANE, blocks * WINDOW))


def line_filters(matrix):
    table = matrix.reshape(18, 2, 9).transpose(1, 0, 2).reshape(2, 162)
    return np.broadcast_to(table[:, :, None], (2, 162, LANES)).astype(np.float32)


def tables():
    matrix, quad = wavelet_tables()
    rows = matrix.reshape(2, 9, 2, 9)
    points = np.einsum("aiop,gp->aiog", rows, quad)
    result = {"line1": line_filters(rows), "line2": line_filters(points)}
    for name, filters in (("plane1", rows), ("plane2", points)):
        high, low = plane_filters(filters, 4, 1)
        result[name] = np.concatenate([high[0], low[0]], 1)
    high, low = plane_filters(points, 1, 9)
    result["plane3"] = np.concatenate([high, high, low], 2)
    return result


def dot(left, right):
    return jnp.dot(left, right, preferred_element_type=jnp.float32)


def spill_selectors():
    row = lax.broadcasted_iota(jnp.int32, (LANES, LANES), 0)
    column = lax.broadcasted_iota(jnp.int32, (LANES, LANES), 1)
    return [
        jnp.where((row - (BOX_DEV - SPILL) == column - SPILL * k) & (row >= BOX_DEV - SPILL), 1.0, 0.0).astype(
            jnp.bfloat16
        )
        for k in range(4)
    ]


def parent_selectors(relative):
    slots = relative.shape[1]
    parent = relative >> 3
    row = lax.broadcasted_iota(jnp.int32, (2 * LANES, slots), 0)
    return [
        jnp.where(row == jnp.where(parent >= 0, parent, parent + BOX_DEV + SPILL * (k + 1)), 1.0, 0.0).astype(
            jnp.bfloat16
        )
        for k in range(4)
    ]


def pack_coarse_kernel(coarse_ref, out_ref, total_ref):
    selectors = spill_selectors()
    total = dot(coarse_ref[0:PART], selectors[0])
    for k in range(1, 3):
        total += dot(coarse_ref[PART * k : PART * (k + 1)], selectors[k])
    total_ref[...] = total
    total_ref[0 : ROWS - 3 * PART] += dot(coarse_ref[3 * PART : ROWS], selectors[3])
    out_ref[...] = total_ref[...].astype(jnp.bfloat16)


def pack_wavelets_kernel(wavelet_ref, leaf_ref, after_ref, out_ref):
    keep = (1 - leaf_ref[...]).astype(jnp.float32)
    selectors = spill_selectors()
    for group in range(2):
        total = None
        for k in range(4):
            block = 4 * group + k
            if block > 0:
                term = dot((wavelet_ref[0, block - 1].astype(jnp.float32) * keep).astype(jnp.bfloat16), selectors[k])
                total = term if total is None else total + term
        out_ref[group] = total.astype(jnp.bfloat16)


def choose_plane(planes, octant):
    upper, right = ((octant >> 1) & 1) == 1, (octant & 1) == 1
    parts = [planes[PLANE * k : PLANE * (k + 1)] for k in range(4)]
    return jnp.where(upper, jnp.where(right, parts[3], parts[2]), jnp.where(right, parts[1], parts[0]))


def line_coefficients(octant, line_ref, coef_ref):
    slots = octant.shape[1]
    for part in range(slots // LANES):
        lanes = slice(LANES * part, LANES * (part + 1))
        coef_ref[0:162, lanes] = jnp.where((octant[:, lanes] >> 2) == 1, line_ref[1], line_ref[0])


def planes_of_blocks(window, plane_ref, octant, chosen_ref):
    slots = octant.shape[1]
    both = jnp.concatenate([octant, octant], axis=1)
    for i in range(9):
        halves = [jnp.concatenate([window(4 * a + k, i) for k in range(4)], axis=0) for a in range(2)]
        data = jnp.concatenate(halves, axis=1)
        planes = dot(plane_ref[...], jnp.concatenate([data, data], axis=0))
        chosen = choose_plane(planes, both)
        chosen_ref[i] = chosen[:, :slots]
        chosen_ref[9 + i] = chosen[:, slots:]


def line_sum(p, count, coef_ref, chosen_ref, start):
    total = start
    for index in range(count):
        row = index * 9 + p
        term = coef_ref[row : row + 1] * chosen_ref[index]
        total = term if total is None else total + term
    return total


def level1_kernel(coarse_ref, halo_ref, relative_ref, plane_ref, line_ref, after_ref, pair_ref, spill_ref, wide_ref, chosen_ref, coef_ref, box_ref):
    relative = relative_ref[...]
    octant = relative & 7
    selectors = parent_selectors(relative)
    wide_ref[ROWS : 8 * TALL] = jnp.zeros((8 * TALL - ROWS, BOX_DEV), jnp.float32)
    for k in range(4):
        start, stop = PART * k, min(PART * (k + 1), ROWS)
        both = jnp.concatenate([coarse_ref[start:stop], halo_ref[0 : stop - start]], axis=1)
        wide_ref[start:stop] = dot(both, selectors[k])
    line_coefficients(octant, line_ref, coef_ref)

    def window(block, i):
        return wide_ref[pl.ds(8 * 81 * i + block, WINDOW, stride=8)].astype(jnp.bfloat16)

    planes_of_blocks(window, plane_ref, octant, chosen_ref)
    box_ref[728:768] = jnp.zeros((40, BOX_DEV), jnp.float32)
    for p in range(9):
        box_ref[81 * p : 81 * p + PLANE] = line_sum(p, 18, coef_ref, chosen_ref, None)
    scaling = box_ref[...]
    high = scaling.astype(jnp.bfloat16)
    low = (scaling - high.astype(jnp.float32)).astype(jnp.bfloat16)
    spill = spill_selectors()
    for index, part in enumerate((high, low)):
        pair_ref[index] = part
        total = dot(part[0:192], spill[0])
        for k in range(1, 4):
            total += dot(part[192 * k : 192 * (k + 1)], spill[k])
        spill_ref[index] = total.astype(jnp.bfloat16)


def own_wavelet_kernel(wavelet_ref, leaf_ref, relative_ref, plane_ref, line_ref, after_ref, out_ref, wide_ref, chosen_ref, coef_ref):
    relative = relative_ref[...]
    octant = relative & 7
    keep = (1 - leaf_ref[...]).astype(jnp.float32)
    row = lax.broadcasted_iota(jnp.int32, (BOX_DEV, SLOTS), 0)
    selector = jnp.where(row == relative >> 3, 1.0, 0.0).astype(jnp.bfloat16)
    for block in range(1, 8):
        own = (wavelet_ref[0, block - 1].astype(jnp.float32) * keep).astype(jnp.bfloat16)
        wide_ref[block, 728:TALL] = jnp.zeros((TALL - 728, SLOTS), jnp.float32)
        wide_ref[block, 0:729] = dot(own, selector)
    line_coefficients(octant, line_ref, coef_ref)
    planes_of_blocks(wavelet_window(wide_ref), plane_ref, octant, chosen_ref)
    for p in range(9):
        out_ref[p] = line_sum(p, 18, coef_ref, chosen_ref, None)


def wavelet_window(wide_ref):
    def window(block, i):
        if block == 0:
            return jnp.zeros((WINDOW, wide_ref.shape[2]), jnp.bfloat16)
        return wide_ref[block, 81 * i : 81 * i + WINDOW].astype(jnp.bfloat16)

    return window


def spill_wavelet_kernel(halo_ref, relative_ref, plane_ref, line_ref, own_ref, after_ref, out_ref, wide_ref, chosen_ref, coef_ref):
    for part in range(SLOTS // LANES):
        lanes = slice(LANES * part, LANES * (part + 1))
        relative = relative_ref[:, lanes]
        spilled = jnp.min(relative) < 0

        @pl.when(spilled)
        def _():
            octant = relative & 7
            parent = (relative >> 3) + SPILL
            row = lax.broadcasted_iota(jnp.int32, (LANES, LANES), 0)
            for block in range(1, 8):
                wanted = jnp.where((parent >= 0) & (parent < SPILL), parent + SPILL * (block % 4), -1)
                selector = jnp.where(row == wanted, 1.0, 0.0).astype(jnp.bfloat16)
                wide_ref[block, 728:TALL] = jnp.zeros((TALL - 728, LANES), jnp.float32)
                wide_ref[block, 0:729] = dot(halo_ref[block // 4], selector)
            line_coefficients(octant, line_ref, coef_ref)
            planes_of_blocks(wavelet_window(wide_ref), plane_ref, octant, chosen_ref)
            for p in range(9):
                out_ref[p, :, lanes] = line_sum(p, 18, coef_ref, chosen_ref, own_ref[p, :, lanes])

        @pl.when(jnp.logical_not(spilled))
        def _():
            out_ref[:, :, lanes] = own_ref[:, :, lanes]


def encode(values, code_ref, targets, largest_ref, scale_ref, power_ref):
    row = lax.broadcasted_iota(jnp.int32, (CHUNK, SLOTS), 0)
    for index, value in enumerate(values):
        largest_ref[index : index + 1] = jnp.max(jnp.where(row < HELD, value(), 0.0), axis=0, keepdims=True)
    largest = largest_ref[...]
    scale = jnp.full(largest.shape, 2.0**-16, jnp.float32)
    power = jnp.zeros(largest.shape, jnp.int32)
    for step in STEPS:
        longer = scale * 2.0**step
        fits = largest * longer < 32766.0
        scale = jnp.where(fits, longer, scale)
        power = jnp.where(fits, power + step, power)
    scale_ref[...] = scale
    power_ref[...] = power
    for index, value in enumerate(values):
        code = jnp.round(value() * scale_ref[index : index + 1]).astype(jnp.int32)
        code = jnp.where(row < HELD, code, power_ref[index : index + 1]).astype(jnp.int16)
        for target in targets(index):
            code_ref[target] = code


def decode_scales(code_ref, power_ref):
    for index in range(CHUNKS):
        tail = code_ref[index, CHUNK - 16 : CHUNK].astype(jnp.int32)
        power_ref[index : index + 1] = tail[15:16]
    power = power_ref[...]
    scale = jnp.full(power.shape, 2.0**16, jnp.float32)
    for step in STEPS:
        taken = power >= step
        scale = jnp.where(taken, scale * 2.0**-step, scale)
        power = jnp.where(taken, power - step, power)
    return scale


def density_kernel(pair_ref, halo_ref, relative_ref, count_ref, plane_ref, line_ref, before_ref, code_ref, gathered_ref, chosen_ref, coef_ref, dense_ref, largest_ref, scale_ref, power_ref):
    relative = relative_ref[...]
    octant = relative & 7
    selectors = parent_selectors(relative)
    for index in range(2):
        for k in range(4):
            rows = slice(192 * k, 192 * (k + 1))
            both = jnp.concatenate([pair_ref[index, rows], halo_ref[index]], axis=1)
            gathered_ref[index, rows] = dot(both, selectors[k]).astype(jnp.bfloat16)
    line_coefficients(octant, line_ref, coef_ref)
    for i in range(9):
        rows = slice(80 * i, 80 * i + WINDOW)
        high = gathered_ref[0, rows]
        planes = dot(plane_ref[i], jnp.concatenate([high, gathered_ref[1, rows], high], axis=0))
        chosen_ref[i] = choose_plane(planes, octant)
    slot = lax.broadcasted_iota(jnp.int32, (1, SLOTS), 1)
    factor = jnp.where(slot < count_ref[0, 0], 2.0, 0.0)
    dense_ref[728:744] = jnp.zeros((16, SLOTS), jnp.float32)
    for p in range(9):
        value = line_sum(p, 9, coef_ref, chosen_ref, before_ref[p])
        dense_ref[81 * p : 81 * p + PLANE] = value * value * factor
    chunks = [lambda c=c: dense_ref[HELD * c : HELD * c + CHUNK] for c in range(CHUNKS)]
    encode(chunks, code_ref, lambda index: (index,), largest_ref, scale_ref, power_ref)


def add_kernel(code_ref, out_ref, power_ref, inverse_ref, total_ref, largest_ref, scale_ref, shared_ref):
    inverse_ref[...] = decode_scales(code_ref, power_ref)
    total = None
    for index in range(CHUNKS):
        term = code_ref[index].astype(jnp.int32).astype(jnp.float32) * inverse_ref[index : index + 1]
        total = term if total is None else total + term
    total_ref[...] = total
    encode([lambda: total_ref[...]], out_ref, lambda index: (slice(None),), largest_ref, scale_ref, shared_ref)


def finish_kernel(code_ref, out_ref, power_ref, inverse_ref):
    inverse_ref[...] = decode_scales(code_ref, power_ref)
    for index in range(CHUNKS):
        rows = min(HELD, 729 - HELD * index)
        value = code_ref[index].astype(jnp.int32).astype(jnp.float32) * inverse_ref[index : index + 1]
        out_ref[HELD * index : HELD * index + rows] = value[0:rows]


def call(kernel, outs, scratch, *operands, scalar=(), apart=()):
    spaces = [pltpu.VMEM] * len(operands)
    for index in scalar:
        spaces[index] = pltpu.SMEM
    for index in apart:
        spaces[index] = pl.ANY
    return pl.pallas_call(
        kernel,
        out_shape=outs,
        in_specs=[pl.BlockSpec(memory_space=space) for space in spaces],
        out_specs=jax.tree.map(lambda out: pl.BlockSpec(memory_space=pltpu.VMEM), outs),
        scratch_shapes=[pltpu.VMEM(shape, kind) for shape, kind in scratch],
        compiler_params=pltpu.CompilerParams(vmem_limit_bytes=VMEM_BYTES),
    )(*operands)


def struct(shape, kind):
    return jax.ShapeDtypeStruct(shape, kind)


def pack_coarse(coarse):
    return call(
        pack_coarse_kernel, struct((PART, LANES), jnp.bfloat16), [((PART, LANES), jnp.float32)], coarse
    )


def pack_wavelets(wavelets, leaf_flags, after):
    return call(
        pack_wavelets_kernel, struct((2, 729, LANES), jnp.bfloat16), [], wavelets, leaf_flags, after, apart=(2,)
    )


def level1(coarse, halo, relative1, table, after):
    return call(
        level1_kernel,
        [struct((2, 768, BOX_DEV), jnp.bfloat16), struct((2, 192, LANES), jnp.bfloat16)],
        [
            ((8 * TALL, BOX_DEV), jnp.float32),
            ((18, PLANE, BOX_DEV), jnp.float32),
            ((168, BOX_DEV), jnp.float32),
            ((768, BOX_DEV), jnp.float32),
        ],
        coarse, halo, relative1, table["plane1"], table["line1"], after, apart=(5,),
    )


def own_wavelets(wavelets, leaf_flags, relative2, table, after):
    return call(
        own_wavelet_kernel,
        struct((9, PLANE, SLOTS), jnp.float32),
        [((8, TALL, SLOTS), jnp.float32), ((18, PLANE, SLOTS), jnp.float32), ((168, SLOTS), jnp.float32)],
        wavelets, leaf_flags, relative2, table["plane2"], table["line2"], after, apart=(5,),
    )


def spill_wavelets(halo, relative2, table, own, after):
    return call(
        spill_wavelet_kernel,
        struct((9, PLANE, SLOTS), jnp.float32),
        [((8, TALL, LANES), jnp.float32), ((18, PLANE, LANES), jnp.float32), ((168, LANES), jnp.float32)],
        halo, relative2, table["plane2"], table["line2"], own, after, apart=(5,),
    )


def density_codes(pair, halo, relative2, counts, table, before):
    return call(
        density_kernel,
        struct((CHUNKS, CHUNK, SLOTS), jnp.int16),
        [
            ((2, 768, SLOTS), jnp.bfloat16),
            ((9, PLANE, SLOTS), jnp.float32),
            ((168, SLOTS), jnp.float32),
            ((744, SLOTS), jnp.float32),
            ((CHUNKS, SLOTS), jnp.float32),
            ((CHUNKS, SLOTS), jnp.float32),
            ((CHUNKS, SLOTS), jnp.int32),
        ],
        pair, halo, relative2, counts, table["plane3"], table["line2"], before, scalar=(3,),
    )


def add_codes(codes):
    return call(
        add_kernel,
        struct((CHUNK, SLOTS), jnp.int16),
        [
            ((CHUNKS, SLOTS), jnp.int32),
            ((CHUNKS, SLOTS), jnp.float32),
            ((CHUNK, SLOTS), jnp.float32),
            ((1, SLOTS), jnp.float32),
            ((1, SLOTS), jnp.float32),
            ((1, SLOTS), jnp.int32),
        ],
        codes,
    )


def finish(codes):
    return call(
        finish_kernel,
        struct((729, SLOTS), jnp.float32),
        [((CHUNKS, SLOTS), jnp.int32), ((CHUNKS, SLOTS), jnp.float32)],
        codes,
    )


def shards(table, coarse, wavelets, leaf_flags, child_key1, child_key2, counts):
    position = lax.axis_index("box")
    relative1 = (child_key1 - position * (8 * BOX_DEV)).reshape(1, BOX_DEV)
    relative2 = (child_key2 - position * (8 * BOX_DEV)).reshape(1, SLOTS)
    coarse = coarse[0].transpose(1, 0, 2).reshape(ROWS, BOX_DEV)
    packed = pack_coarse(coarse)
    coarse_halo = shifted_2(packed, "box", 1)
    packed = pack_wavelets(wavelets, leaf_flags, packed)
    wavelet_halo = shifted_2(packed, "box", 1)
    own = own_wavelets(wavelets, leaf_flags, relative2, table, packed)
    pair, spill = level1(coarse, coarse_halo, relative1, table, own)
    pair_halo = shifted_2(spill, "box", 1)
    before = spill_wavelets(wavelet_halo, relative2, table, own, spill)
    codes = density_codes(pair, pair_halo, relative2, counts.reshape(1, 1), table, before)
    codes = lax.all_to_all(codes, "orb", 0, 0, tiled=True)
    return finish(lax.all_gather(add_codes(codes), "orb"))


def solution(mesh):
    in_specs = (
        P("orb", None, None, "box"),
        P("orb", None, None, "box"),
        P("orb", "box"),
        P("box"),
        P("box"),
        P("box"),
    )
    out_specs = P(None, "box")
    table = {name: jnp.asarray(value) for name, value in tables().items()}
    local = functools.partial(shards, table)
    return jax.shard_map(local, mesh=mesh, in_specs=in_specs, out_specs=out_specs, check_vma=False)
```

```python
import functools
import math

import jax
import jax.numpy as jnp
import numpy as np
from jax import lax
from jax.experimental import pallas as pl
from jax.experimental.pallas import tpu as pltpu
from jax.sharding import Mesh
from jax.sharding import PartitionSpec as P

BOX_DEV = 128
SPILL = 32
SLOTS = 256
LANES = 128
PLANE = 88
WINDOW = 96
ROWS = 8 * 729
PART = 1472
TALL = 744
SPILL_ROWS = 1296
CHUNKS = 16
CHUNK = 48
HELD = 46
STEPS = (64, 32, 16, 8, 8, 4, 2, 1)
VMEM_BYTES = 20 * 1024 * 1024


def shifted_2(value, axis, steps):
    count = lax.axis_size(axis)
    first, last = (max(0, -steps), min(count, count - steps))
    return lax.ppermute(value, axis, [(source, source + steps) for source in range(first, last)])


def legendre_pair(order, where):
    before = where * 0.0 + 1.0
    value = where
    for degree in range(1, order):
        before, value = (value, ((2 * degree + 1) * where * value - degree * before) / (degree + 1))
    return (value, before)


def gauss_rule(order):
    nodes = np.cos(np.pi * (np.arange(order) + 0.75) / (order + 0.5))
    for repeat in range(40):
        value, before = legendre_pair(order, nodes)
        slope = order * (nodes * value - before) / (nodes * nodes - 1.0)
        nodes = nodes - value / slope
    value, before = legendre_pair(order, nodes)
    slope = order * (nodes * value - before) / (nodes * nodes - 1.0)
    weights = 2.0 / ((1.0 - nodes * nodes) * slope * slope)
    return (nodes[::-1], weights[::-1])


def legendre_basis(where):
    shifted = 2.0 * where - 1.0
    rows = [shifted * 0.0 + 1.0, shifted]
    for degree in range(1, 8):
        rows.append(
            ((2 * degree + 1) * shifted * rows[degree] - degree * rows[degree - 1]) / (degree + 1)
        )
    scale = np.sqrt(2.0 * np.arange(9) + 1.0)[:, None]
    return np.stack(rows, 0) * scale


def complement_rows(scaling_rows):
    members = [scaling_rows[index] for index in range(9)]
    kept = []
    identity = np.eye(18)
    for column in range(18):
        vector = identity[column]
        for passes in range(2):
            for member in members + kept:
                vector = vector - np.dot(member, vector) * member
        length = np.sqrt(np.dot(vector, vector))
        if length > 0.1 and len(kept) < 9:
            kept.append(vector / length)
    return np.stack(kept, 0)


def wavelet_tables():
    nodes, weights = gauss_rule(24)
    points = 0.5 * (nodes + 1.0)
    halves = 0.5 * weights
    lower = legendre_basis(0.5 * points) * halves @ legendre_basis(points).T / math.sqrt(2.0)
    upper = legendre_basis(0.5 * points + 0.5) * halves @ legendre_basis(points).T / math.sqrt(2.0)
    scaling_rows = np.concatenate([lower, upper], 1)
    wavelet_rows = complement_rows(scaling_rows)
    matrix = np.concatenate([scaling_rows, wavelet_rows], 0).reshape(2, 9, 2, 9)
    gauss, gauss_weights = gauss_rule(9)
    quad = legendre_basis(0.5 * (gauss + 1.0)).T * np.sqrt(0.5 * gauss_weights)[:, None]
    return (matrix, quad)


def bf16_pair(table):
    high = table.astype(np.float32).astype(jnp.bfloat16)
    low = (table - high.astype(np.float64)).astype(np.float32).astype(jnp.bfloat16)
    return (high, low)


def plane_filters(matrix, blocks, shifts):
    plane = np.einsum("bjqe,clrf->qrefbcjl", matrix, matrix).reshape(4, 81, 4, 81)[:, :, :blocks]
    tables = np.zeros((shifts, 4, PLANE, blocks, WINDOW))
    for index in range(shifts):
        tables[index, :, :81, :, index : index + 81] = plane
    return bf16_pair(tables.reshape(shifts, 4 * PLANE, blocks * WINDOW))


def line_filters(matrix):
    table = matrix.reshape(18, 2, 9).transpose(1, 0, 2).reshape(2, 162)
    return np.broadcast_to(table[:, :, None], (2, 162, LANES)).astype(np.float32)


def tables():
    matrix, quad = wavelet_tables()
    rows = matrix.reshape(2, 9, 2, 9)
    points = np.einsum("aiop,gp->aiog", rows, quad)
    result = {"line1": line_filters(rows), "line2": line_filters(points)}
    for name, filters in (("plane1", rows), ("plane2", points)):
        high, low = plane_filters(filters, 4, 1)
        result[name] = np.concatenate([high[0], low[0]], 1)
    high, low = plane_filters(points, 1, 9)
    result["plane3"] = np.concatenate([high, high, low], 2)
    return result


def dot(left, right):
    return jnp.dot(left, right, preferred_element_type=jnp.float32)


def spill_selectors():
    row = lax.broadcasted_iota(jnp.int32, (LANES, LANES), 0)
    column = lax.broadcasted_iota(jnp.int32, (LANES, LANES), 1)
    return [
        jnp.where((row - (BOX_DEV - SPILL) == column - SPILL * k) & (row >= BOX_DEV - SPILL), 1.0, 0.0).astype(
            jnp.bfloat16
        )
        for k in range(4)
    ]


def parent_selectors(relative):
    slots = relative.shape[1]
    parent = relative >> 3
    row = lax.broadcasted_iota(jnp.int32, (2 * LANES, slots), 0)
    return [
        jnp.where(row == jnp.where(parent >= 0, parent, parent + BOX_DEV + SPILL * (k + 1)), 1.0, 0.0).astype(
            jnp.bfloat16
        )
        for k in range(4)
    ]


def pack_coarse_kernel(coarse_ref, out_ref, total_ref):
    selectors = spill_selectors()
    total = dot(coarse_ref[0:PART], selectors[0])
    for k in range(1, 3):
        total += dot(coarse_ref[PART * k : PART * (k + 1)], selectors[k])
    total_ref[...] = total
    total_ref[0 : ROWS - 3 * PART] += dot(coarse_ref[3 * PART : ROWS], selectors[3])
    out_ref[...] = total_ref[...].astype(jnp.bfloat16)


def wavelet_segments():
    tiles, segments = SPILL_ROWS // 16, []
    for group in range(4):
        for block in range(1, 8):
            first, last = max(46 * (block - 1), tiles * group), min(46 * block, tiles * (group + 1))
            if first < last:
                segments.append((block, 16 * (first - 46 * (block - 1)), 16 * (last - first), group, 16 * (first - tiles * group)))
    return segments


def pack_wavelets_kernel(wavelet_ref, leaf_ref, after_ref, out_ref, total_ref):
    keep = (1 - leaf_ref[...]).astype(jnp.float32)
    selectors = spill_selectors()
    total_ref[...] = jnp.zeros((SPILL_ROWS, LANES), jnp.float32)
    for block, row, rows, group, target in wavelet_segments():
        rows = min(rows, 729 - row)
        part = (wavelet_ref[0, block - 1, row : row + rows].astype(jnp.float32) * keep).astype(jnp.bfloat16)
        total_ref[target : target + rows] += dot(part, selectors[group])
    out_ref[...] = total_ref[...].astype(jnp.bfloat16)


def choose_plane(planes, octant):
    upper, right = ((octant >> 1) & 1) == 1, (octant & 1) == 1
    parts = [planes[PLANE * k : PLANE * (k + 1)] for k in range(4)]
    return jnp.where(upper, jnp.where(right, parts[3], parts[2]), jnp.where(right, parts[1], parts[0]))


def line_coefficients(octant, line_ref, coef_ref):
    slots = octant.shape[1]
    for part in range(slots // LANES):
        lanes = slice(LANES * part, LANES * (part + 1))
        coef_ref[0:162, lanes] = jnp.where((octant[:, lanes] >> 2) == 1, line_ref[1], line_ref[0])


def planes_of_blocks(window, plane_ref, octant, chosen_ref):
    slots = octant.shape[1]
    both = jnp.concatenate([octant, octant], axis=1)
    for i in range(9):
        halves = [jnp.concatenate([window(4 * a + k, i) for k in range(4)], axis=0) for a in range(2)]
        data = jnp.concatenate(halves, axis=1)
        planes = dot(plane_ref[...], jnp.concatenate([data, data], axis=0))
        chosen = choose_plane(planes, both)
        chosen_ref[i] = chosen[:, :slots]
        chosen_ref[9 + i] = chosen[:, slots:]


def line_sum(p, count, coef_ref, chosen_ref, start):
    total = start
    for index in range(count):
        row = index * 9 + p
        term = coef_ref[row : row + 1] * chosen_ref[index]
        total = term if total is None else total + term
    return total


def level1_kernel(coarse_ref, halo_ref, relative_ref, plane_ref, line_ref, after_ref, pair_ref, spill_ref, wide_ref, chosen_ref, coef_ref, box_ref):
    relative = relative_ref[...]
    octant = relative & 7
    selectors = parent_selectors(relative)
    wide_ref[ROWS : 8 * TALL] = jnp.zeros((8 * TALL - ROWS, BOX_DEV), jnp.float32)
    for k in range(4):
        start, stop = PART * k, min(PART * (k + 1), ROWS)
        both = jnp.concatenate([coarse_ref[start:stop], halo_ref[0 : stop - start]], axis=1)
        wide_ref[start:stop] = dot(both, selectors[k])
    line_coefficients(octant, line_ref, coef_ref)

    def window(block, i):
        return wide_ref[pl.ds(8 * 81 * i + block, WINDOW, stride=8)].astype(jnp.bfloat16)

    planes_of_blocks(window, plane_ref, octant, chosen_ref)
    box_ref[728:768] = jnp.zeros((40, BOX_DEV), jnp.float32)
    for p in range(9):
        box_ref[81 * p : 81 * p + PLANE] = line_sum(p, 18, coef_ref, chosen_ref, None)
    scaling = box_ref[...]
    high = scaling.astype(jnp.bfloat16)
    low = (scaling - high.astype(jnp.float32)).astype(jnp.bfloat16)
    spill = spill_selectors()
    for index, part in enumerate((high, low)):
        pair_ref[index] = part
        total = dot(part[0:192], spill[0])
        for k in range(1, 4):
            total += dot(part[192 * k : 192 * (k + 1)], spill[k])
        spill_ref[index] = total.astype(jnp.bfloat16)


def own_wavelet_kernel(wavelet_ref, leaf_ref, relative_ref, plane_ref, line_ref, after_ref, out_ref, wide_ref, chosen_ref, coef_ref):
    relative = relative_ref[...]
    octant = relative & 7
    keep = (1 - leaf_ref[...]).astype(jnp.float32)
    row = lax.broadcasted_iota(jnp.int32, (BOX_DEV, SLOTS), 0)
    selector = jnp.where(row == relative >> 3, 1.0, 0.0).astype(jnp.bfloat16)
    for block in range(1, 8):
        own = (wavelet_ref[0, block - 1].astype(jnp.float32) * keep).astype(jnp.bfloat16)
        wide_ref[block, 728:TALL] = jnp.zeros((TALL - 728, SLOTS), jnp.float32)
        wide_ref[block, 0:729] = dot(own, selector)
    line_coefficients(octant, line_ref, coef_ref)
    planes_of_blocks(wavelet_window(wide_ref), plane_ref, octant, chosen_ref)
    for p in range(9):
        out_ref[p] = line_sum(p, 18, coef_ref, chosen_ref, None)


def wavelet_window(wide_ref):
    def window(block, i):
        if block == 0:
            return jnp.zeros((WINDOW, wide_ref.shape[2]), jnp.bfloat16)
        return wide_ref[block, 81 * i : 81 * i + WINDOW].astype(jnp.bfloat16)

    return window


def spill_wavelet_kernel(halo_ref, relative_ref, plane_ref, line_ref, own_ref, after_ref, out_ref, wide_ref, chosen_ref, coef_ref):
    for part in range(SLOTS // LANES):
        lanes = slice(LANES * part, LANES * (part + 1))
        relative = relative_ref[:, lanes]
        spilled = jnp.min(relative) < 0

        @pl.when(spilled)
        def _():
            octant = relative & 7
            parent = (relative >> 3) + SPILL
            row = lax.broadcasted_iota(jnp.int32, (LANES, LANES), 0)
            selectors = []
            for group in range(4):
                wanted = jnp.where((parent >= 0) & (parent < SPILL), parent + SPILL * group, -1)
                selectors.append(jnp.where(row == wanted, 1.0, 0.0).astype(jnp.bfloat16))
            for block in range(1, 8):
                wide_ref[block, 736:TALL] = jnp.zeros((TALL - 736, LANES), jnp.float32)
            for block, first, rows, group, place in wavelet_segments():
                wide_ref[block, first : first + rows] = dot(halo_ref[place : place + rows], selectors[group])
            line_coefficients(octant, line_ref, coef_ref)
            planes_of_blocks(wavelet_window(wide_ref), plane_ref, octant, chosen_ref)
            for p in range(9):
                out_ref[p, :, lanes] = line_sum(p, 18, coef_ref, chosen_ref, own_ref[p, :, lanes])

        @pl.when(jnp.logical_not(spilled))
        def _():
            out_ref[:, :, lanes] = own_ref[:, :, lanes]


def encode(values, code_ref, targets, largest_ref, scale_ref, power_ref):
    row = lax.broadcasted_iota(jnp.int32, (CHUNK, SLOTS), 0)
    for index, value in enumerate(values):
        largest_ref[index : index + 1] = jnp.max(jnp.where(row < HELD, value(), 0.0), axis=0, keepdims=True)
    largest = largest_ref[...]
    scale = jnp.full(largest.shape, 2.0**-16, jnp.float32)
    power = jnp.zeros(largest.shape, jnp.int32)
    for step in STEPS:
        longer = scale * 2.0**step
        fits = largest * longer < 32766.0
        scale = jnp.where(fits, longer, scale)
        power = jnp.where(fits, power + step, power)
    scale_ref[...] = scale
    power_ref[...] = power
    for index, value in enumerate(values):
        code = jnp.round(value() * scale_ref[index : index + 1]).astype(jnp.int32)
        code = jnp.where(row < HELD, code, power_ref[index : index + 1]).astype(jnp.int16)
        for target in targets(index):
            code_ref[target] = code


def decode_scales(code_ref, power_ref):
    for index in range(code_ref.shape[0]):
        tail = code_ref[index, CHUNK - 16 : CHUNK].astype(jnp.int32)
        power_ref[index : index + 1] = tail[15:16]
    power = power_ref[...]
    scale = jnp.full(power.shape, 2.0**16, jnp.float32)
    for step in STEPS:
        taken = power >= step
        scale = jnp.where(taken, scale * 2.0**-step, scale)
        power = jnp.where(taken, power - step, power)
    return scale


def density_kernel(pair_ref, halo_ref, relative_ref, count_ref, plane_ref, line_ref, before_ref, code_ref, gathered_ref, chosen_ref, coef_ref, dense_ref, largest_ref, scale_ref, power_ref):
    relative = relative_ref[...]
    octant = relative & 7
    selectors = parent_selectors(relative)
    spilled = jnp.concatenate([halo_ref[0], halo_ref[1]], axis=0)
    for k in range(4):
        rows = slice(192 * k, 192 * (k + 1))
        own = jnp.concatenate([pair_ref[0, rows], pair_ref[1, rows]], axis=0)
        both = dot(jnp.concatenate([own, spilled], axis=1), selectors[k]).astype(jnp.bfloat16)
        gathered_ref[0, rows] = both[0:192]
        gathered_ref[1, rows] = both[192:384]
    line_coefficients(octant, line_ref, coef_ref)
    for i in range(9):
        rows = slice(80 * i, 80 * i + WINDOW)
        high = gathered_ref[0, rows]
        planes = dot(plane_ref[i], jnp.concatenate([high, gathered_ref[1, rows], high], axis=0))
        chosen_ref[i] = choose_plane(planes, octant)
    slot = lax.broadcasted_iota(jnp.int32, (1, SLOTS), 1)
    factor = jnp.where(slot < count_ref[0, 0], 2.0, 0.0)
    dense_ref[728:744] = jnp.zeros((16, SLOTS), jnp.float32)
    for p in range(9):
        value = line_sum(p, 9, coef_ref, chosen_ref, before_ref[p])
        dense_ref[81 * p : 81 * p + PLANE] = value * value * factor
    chunks = [lambda c=c: dense_ref[HELD * c : HELD * c + CHUNK] for c in range(CHUNKS)]
    encode(chunks, code_ref, lambda index: (index,), largest_ref, scale_ref, power_ref)


def pair_kernel(core_ref, own_ref, got_ref, out_ref, power_ref, inverse_ref, total_ref, largest_ref, scale_ref, shared_ref):
    half = pl.ds(core_ref[0, 0] * (CHUNKS // 2), CHUNKS // 2)
    pieces = [own_ref.at[half], got_ref.at[half]]
    for part, code_ref in enumerate(pieces):
        inverse_ref[part] = decode_scales(code_ref, power_ref)
    for index in range(CHUNKS // 2):
        total = None
        for part, code_ref in enumerate(pieces):
            term = code_ref[index].astype(jnp.int32).astype(jnp.float32) * inverse_ref[part, index : index + 1]
            total = term if total is None else total + term
        total_ref[index] = total
    chunks = [lambda c=c: total_ref[c] for c in range(CHUNKS // 2)]
    encode(chunks, out_ref, lambda index: (index,), largest_ref, scale_ref, shared_ref)


def add_kernel(code_ref, out_ref, power_ref, inverse_ref, total_ref, largest_ref, scale_ref, shared_ref):
    inverse_ref[...] = decode_scales(code_ref, power_ref)
    total = None
    for index in range(CHUNKS // 2):
        term = code_ref[index].astype(jnp.int32).astype(jnp.float32) * inverse_ref[index : index + 1]
        total = term if total is None else total + term
    total_ref[...] = total
    encode([lambda: total_ref[...]], out_ref, lambda index: range(CHUNKS // 2), largest_ref, scale_ref, shared_ref)


def finish_kernel(code_ref, out_ref, power_ref, inverse_ref):
    inverse_ref[...] = decode_scales(code_ref, power_ref)
    for index in range(CHUNKS):
        rows = min(HELD, 729 - HELD * index)
        value = code_ref[index].astype(jnp.int32).astype(jnp.float32) * inverse_ref[index : index + 1]
        out_ref[HELD * index : HELD * index + rows] = value[0:rows]


def call(kernel, outs, scratch, *operands, scalar=(), apart=()):
    spaces = [pltpu.VMEM] * len(operands)
    for index in scalar:
        spaces[index] = pltpu.SMEM
    for index in apart:
        spaces[index] = pl.ANY
    return pl.pallas_call(
        kernel,
        out_shape=outs,
        in_specs=[pl.BlockSpec(memory_space=space) for space in spaces],
        out_specs=jax.tree.map(lambda out: pl.BlockSpec(memory_space=pltpu.VMEM), outs),
        scratch_shapes=[pltpu.VMEM(shape, kind) for shape, kind in scratch],
        compiler_params=pltpu.CompilerParams(vmem_limit_bytes=VMEM_BYTES),
    )(*operands)


def struct(shape, kind):
    return jax.ShapeDtypeStruct(shape, kind)


def pack_coarse(coarse):
    return call(
        pack_coarse_kernel, struct((PART, LANES), jnp.bfloat16), [((PART, LANES), jnp.float32)], coarse
    )


def pack_wavelets(wavelets, leaf_flags, after):
    return call(
        pack_wavelets_kernel,
        struct((SPILL_ROWS, LANES), jnp.bfloat16),
        [((SPILL_ROWS, LANES), jnp.float32)],
        wavelets, leaf_flags, after, apart=(2,),
    )


def level1(coarse, halo, relative1, table, after):
    return call(
        level1_kernel,
        [struct((2, 768, BOX_DEV), jnp.bfloat16), struct((2, 192, LANES), jnp.bfloat16)],
        [
            ((8 * TALL, BOX_DEV), jnp.float32),
            ((18, PLANE, BOX_DEV), jnp.float32),
            ((168, BOX_DEV), jnp.float32),
            ((768, BOX_DEV), jnp.float32),
        ],
        coarse, halo, relative1, table["plane1"], table["line1"], after, apart=(5,),
    )


def own_wavelets(wavelets, leaf_flags, relative2, table, after):
    return call(
        own_wavelet_kernel,
        struct((9, PLANE, SLOTS), jnp.float32),
        [((8, TALL, SLOTS), jnp.float32), ((18, PLANE, SLOTS), jnp.float32), ((168, SLOTS), jnp.float32)],
        wavelets, leaf_flags, relative2, table["plane2"], table["line2"], after, apart=(5,),
    )


def spill_wavelets(halo, relative2, table, own, after):
    return call(
        spill_wavelet_kernel,
        struct((9, PLANE, SLOTS), jnp.float32),
        [((8, TALL, LANES), jnp.float32), ((18, PLANE, LANES), jnp.float32), ((168, LANES), jnp.float32)],
        halo, relative2, table["plane2"], table["line2"], own, after, apart=(5,),
    )


def density_codes(pair, halo, relative2, counts, table, before):
    return call(
        density_kernel,
        struct((CHUNKS, CHUNK, SLOTS), jnp.int16),
        [
            ((2, 768, SLOTS), jnp.bfloat16),
            ((9, PLANE, SLOTS), jnp.float32),
            ((168, SLOTS), jnp.float32),
            ((744, SLOTS), jnp.float32),
            ((CHUNKS, SLOTS), jnp.float32),
            ((CHUNKS, SLOTS), jnp.float32),
            ((CHUNKS, SLOTS), jnp.int32),
        ],
        pair, halo, relative2, counts, table["plane3"], table["line2"], before, scalar=(3,),
    )


def add_pair(core, own, got):
    half = CHUNKS // 2
    return call(
        pair_kernel,
        struct((half, CHUNK, SLOTS), jnp.int16),
        [
            ((half, SLOTS), jnp.int32),
            ((2, half, SLOTS), jnp.float32),
            ((half, CHUNK, SLOTS), jnp.float32),
            ((half, SLOTS), jnp.float32),
            ((half, SLOTS), jnp.float32),
            ((half, SLOTS), jnp.int32),
        ],
        core, own, got, scalar=(0,),
    )


def add_codes(codes):
    return call(
        add_kernel,
        struct((CHUNKS // 2, CHUNK, SLOTS), jnp.int16),
        [
            ((CHUNKS // 2, SLOTS), jnp.int32),
            ((CHUNKS // 2, SLOTS), jnp.float32),
            ((CHUNK, SLOTS), jnp.float32),
            ((1, SLOTS), jnp.float32),
            ((1, SLOTS), jnp.float32),
            ((1, SLOTS), jnp.int32),
        ],
        codes,
    )


def finish(codes):
    return call(
        finish_kernel,
        struct((729, SLOTS), jnp.float32),
        [((CHUNKS, SLOTS), jnp.int32), ((CHUNKS, SLOTS), jnp.float32)],
        codes,
    )


def shards(table, coarse, wavelets, leaf_flags, child_key1, child_key2, counts):
    position = lax.axis_index("box")
    relative1 = (child_key1 - position * (8 * BOX_DEV)).reshape(1, BOX_DEV)
    relative2 = (child_key2 - position * (8 * BOX_DEV)).reshape(1, SLOTS)
    coarse = coarse[0].transpose(1, 0, 2).reshape(ROWS, BOX_DEV)
    packed = pack_coarse(coarse)
    coarse_halo = shifted_2(packed, "box", 1)
    packed = pack_wavelets(wavelets, leaf_flags, packed)
    wavelet_halo = shifted_2(packed, "box", 1)
    own = own_wavelets(wavelets, leaf_flags, relative2, table, packed)
    pair, spill = level1(coarse, coarse_halo, relative1, table, own)
    pair_halo = shifted_2(spill, "box", 1)
    before = spill_wavelets(wavelet_halo, relative2, table, own, spill)
    codes = density_codes(pair, pair_halo, relative2, counts.reshape(1, 1), table, before)
    got = lax.ppermute(codes, "core", [(0, 1), (1, 0)])
    codes = add_pair(lax.axis_index("core").reshape(1, 1), codes, got)
    codes = lax.all_to_all(codes, "z", 0, 0, tiled=True)
    codes = lax.all_to_all(add_codes(codes), "z", 0, 0, tiled=True)
    return finish(lax.all_gather(codes, "core").reshape(CHUNKS, CHUNK, SLOTS))


def solution(mesh):
    orbitals, boxes = mesh.devices.shape
    mesh = Mesh(mesh.devices.reshape(orbitals // 2, 2, boxes), ("z", "core", "box"))
    orb = ("z", "core")
    in_specs = (P(orb, None, None, "box"), P(orb, None, None, "box"), P(orb, "box"), P("box"), P("box"), P("box"))
    out_specs = P(None, "box")
    table = {name: jnp.asarray(value) for name, value in tables().items()}
    local = functools.partial(shards, table)
    return jax.shard_map(local, mesh=mesh, in_specs=in_specs, out_specs=out_specs, check_vma=False)
```

```python
import functools
import math

import jax
import jax.numpy as jnp
import numpy as np
from jax import lax
from jax.experimental import pallas as pl
from jax.experimental.pallas import tpu as pltpu
from jax.sharding import Mesh
from jax.sharding import PartitionSpec as P

BOX_DEV = 128
SPILL = 32
SLOTS = 256
LANES = 128
QUARTER = 64
PLANE = 88
WINDOW = 96
ROWS = 8 * 729
PART = 1472
TALL = 744
SPILL_ROWS = 1296
CHUNKS = 16
CHUNK = 48
HELD = 46
HALF_ROWS = 368
STEPS = (64, 32, 16, 8, 8, 4, 2, 1)
VMEM_BYTES = 20 * 1024 * 1024


def shifted_2(value, axis, steps):
    count = lax.axis_size(axis)
    first, last = (max(0, -steps), min(count, count - steps))
    return lax.ppermute(value, axis, [(source, source + steps) for source in range(first, last)])


def legendre_pair(order, where):
    before = where * 0.0 + 1.0
    value = where
    for degree in range(1, order):
        before, value = (value, ((2 * degree + 1) * where * value - degree * before) / (degree + 1))
    return (value, before)


def gauss_rule(order):
    nodes = np.cos(np.pi * (np.arange(order) + 0.75) / (order + 0.5))
    for repeat in range(40):
        value, before = legendre_pair(order, nodes)
        slope = order * (nodes * value - before) / (nodes * nodes - 1.0)
        nodes = nodes - value / slope
    value, before = legendre_pair(order, nodes)
    slope = order * (nodes * value - before) / (nodes * nodes - 1.0)
    weights = 2.0 / ((1.0 - nodes * nodes) * slope * slope)
    return (nodes[::-1], weights[::-1])


def legendre_basis(where):
    shifted = 2.0 * where - 1.0
    rows = [shifted * 0.0 + 1.0, shifted]
    for degree in range(1, 8):
        rows.append(
            ((2 * degree + 1) * shifted * rows[degree] - degree * rows[degree - 1]) / (degree + 1)
        )
    scale = np.sqrt(2.0 * np.arange(9) + 1.0)[:, None]
    return np.stack(rows, 0) * scale


def complement_rows(scaling_rows):
    members = [scaling_rows[index] for index in range(9)]
    kept = []
    identity = np.eye(18)
    for column in range(18):
        vector = identity[column]
        for passes in range(2):
            for member in members + kept:
                vector = vector - np.dot(member, vector) * member
        length = np.sqrt(np.dot(vector, vector))
        if length > 0.1 and len(kept) < 9:
            kept.append(vector / length)
    return np.stack(kept, 0)


def wavelet_tables():
    nodes, weights = gauss_rule(24)
    points = 0.5 * (nodes + 1.0)
    halves = 0.5 * weights
    lower = legendre_basis(0.5 * points) * halves @ legendre_basis(points).T / math.sqrt(2.0)
    upper = legendre_basis(0.5 * points + 0.5) * halves @ legendre_basis(points).T / math.sqrt(2.0)
    scaling_rows = np.concatenate([lower, upper], 1)
    wavelet_rows = complement_rows(scaling_rows)
    matrix = np.concatenate([scaling_rows, wavelet_rows], 0).reshape(2, 9, 2, 9)
    gauss, gauss_weights = gauss_rule(9)
    quad = legendre_basis(0.5 * (gauss + 1.0)).T * np.sqrt(0.5 * gauss_weights)[:, None]
    return (matrix, quad)


def bf16_pair(table):
    high = table.astype(np.float32).astype(jnp.bfloat16)
    low = (table - high.astype(np.float64)).astype(np.float32).astype(jnp.bfloat16)
    return (high, low)


def plane_filters(matrix, blocks, shifts):
    plane = np.einsum("bjqe,clrf->qrefbcjl", matrix, matrix).reshape(4, 81, 4, 81)[:, :, :blocks]
    tables = np.zeros((shifts, 4, PLANE, blocks, WINDOW))
    for index in range(shifts):
        tables[index, :, :81, :, index : index + 81] = plane
    return bf16_pair(tables.reshape(shifts, 4 * PLANE, blocks * WINDOW))


def line_filters(matrix):
    table = matrix.reshape(18, 2, 9).transpose(1, 0, 2).reshape(2, 162)
    return np.broadcast_to(table[:, :, None], (2, 162, LANES)).astype(np.float32)


def tables():
    matrix, quad = wavelet_tables()
    rows = matrix.reshape(2, 9, 2, 9)
    points = np.einsum("aiop,gp->aiog", rows, quad)
    result = {"line1": line_filters(rows), "line2": line_filters(points)}
    for name, filters in (("plane1", rows), ("plane2", points)):
        high, low = plane_filters(filters, 4, 1)
        result[name] = np.concatenate([high[0], low[0]], 1)
    high, low = plane_filters(points, 1, 9)
    result["plane3"] = np.concatenate([high, high, low], 2)
    return result


def dot(left, right):
    return jnp.dot(left, right, preferred_element_type=jnp.float32)


def spill_selectors():
    row = lax.broadcasted_iota(jnp.int32, (LANES, LANES), 0)
    column = lax.broadcasted_iota(jnp.int32, (LANES, LANES), 1)
    return [
        jnp.where((row - (BOX_DEV - SPILL) == column - SPILL * k) & (row >= BOX_DEV - SPILL), 1.0, 0.0).astype(
            jnp.bfloat16
        )
        for k in range(4)
    ]


def parent_selectors(relative):
    slots = relative.shape[1]
    parent = relative >> 3
    row = lax.broadcasted_iota(jnp.int32, (2 * LANES, slots), 0)
    return [
        jnp.where(row == jnp.where(parent >= 0, parent, parent + BOX_DEV + SPILL * (k + 1)), 1.0, 0.0).astype(
            jnp.bfloat16
        )
        for k in range(4)
    ]


def pack_coarse_kernel(coarse_ref, out_ref, total_ref):
    selectors = spill_selectors()
    total = dot(coarse_ref[0:PART], selectors[0])
    for k in range(1, 3):
        total += dot(coarse_ref[PART * k : PART * (k + 1)], selectors[k])
    total_ref[...] = total
    total_ref[0 : ROWS - 3 * PART] += dot(coarse_ref[3 * PART : ROWS], selectors[3])
    out_ref[...] = total_ref[...].astype(jnp.bfloat16)


def wavelet_segments():
    tiles, segments = SPILL_ROWS // 16, []
    for group in range(4):
        for block in range(1, 8):
            first, last = max(46 * (block - 1), tiles * group), min(46 * block, tiles * (group + 1))
            if first < last:
                segments.append((block, 16 * (first - 46 * (block - 1)), 16 * (last - first), group, 16 * (first - tiles * group)))
    return segments


def pack_wavelets_kernel(wavelet_ref, leaf_ref, after_ref, out_ref, total_ref):
    keep = (1 - leaf_ref[...]).astype(jnp.float32)
    selectors = spill_selectors()
    total_ref[...] = jnp.zeros((SPILL_ROWS, LANES), jnp.float32)
    for block, row, rows, group, target in wavelet_segments():
        rows = min(rows, 729 - row)
        part = (wavelet_ref[0, block - 1, row : row + rows].astype(jnp.float32) * keep).astype(jnp.bfloat16)
        total_ref[target : target + rows] += dot(part, selectors[group])
    out_ref[...] = total_ref[...].astype(jnp.bfloat16)


def choose_plane(planes, octant):
    upper, right = ((octant >> 1) & 1) == 1, (octant & 1) == 1
    parts = [planes[PLANE * k : PLANE * (k + 1)] for k in range(4)]
    return jnp.where(upper, jnp.where(right, parts[3], parts[2]), jnp.where(right, parts[1], parts[0]))


def line_coefficients(octant, line_ref, coef_ref):
    slots = octant.shape[1]
    for part in range(slots // LANES):
        lanes = slice(LANES * part, LANES * (part + 1))
        coef_ref[0:162, lanes] = jnp.where((octant[:, lanes] >> 2) == 1, line_ref[1], line_ref[0])


def planes_of_blocks(window, plane_ref, octant, chosen_ref):
    slots = octant.shape[1]
    both = jnp.concatenate([octant, octant], axis=1)
    for i in range(9):
        halves = [jnp.concatenate([window(4 * a + k, i) for k in range(4)], axis=0) for a in range(2)]
        data = jnp.concatenate(halves, axis=1)
        planes = dot(plane_ref[...], jnp.concatenate([data, data], axis=0))
        chosen = choose_plane(planes, both)
        chosen_ref[i] = chosen[:, :slots]
        chosen_ref[9 + i] = chosen[:, slots:]


def line_sum(p, count, coef_ref, chosen_ref, start):
    total = start
    for index in range(count):
        row = index * 9 + p
        term = coef_ref[row : row + 1] * chosen_ref[index]
        total = term if total is None else total + term
    return total


def level1_kernel(coarse_ref, halo_ref, relative_ref, plane_ref, line_ref, after_ref, pair_ref, spill_ref, wide_ref, chosen_ref, coef_ref, box_ref):
    relative = relative_ref[...]
    octant = relative & 7
    selectors = parent_selectors(relative)
    wide_ref[ROWS : 8 * TALL] = jnp.zeros((8 * TALL - ROWS, BOX_DEV), jnp.float32)
    for k in range(4):
        start, stop = PART * k, min(PART * (k + 1), ROWS)
        both = jnp.concatenate([coarse_ref[start:stop], halo_ref[0 : stop - start]], axis=1)
        wide_ref[start:stop] = dot(both, selectors[k])
    line_coefficients(octant, line_ref, coef_ref)

    def window(block, i):
        return wide_ref[pl.ds(8 * 81 * i + block, WINDOW, stride=8)].astype(jnp.bfloat16)

    planes_of_blocks(window, plane_ref, octant, chosen_ref)
    box_ref[728:768] = jnp.zeros((40, BOX_DEV), jnp.float32)
    for p in range(9):
        box_ref[81 * p : 81 * p + PLANE] = line_sum(p, 18, coef_ref, chosen_ref, None)
    scaling = box_ref[...]
    high = scaling.astype(jnp.bfloat16)
    low = (scaling - high.astype(jnp.float32)).astype(jnp.bfloat16)
    spill = spill_selectors()
    for index, part in enumerate((high, low)):
        pair_ref[index] = part
        total = dot(part[0:192], spill[0])
        for k in range(1, 4):
            total += dot(part[192 * k : 192 * (k + 1)], spill[k])
        spill_ref[index] = total.astype(jnp.bfloat16)


def own_wavelet_kernel(wavelet_ref, leaf_ref, relative_ref, plane_ref, line_ref, after_ref, out_ref, wide_ref, chosen_ref, coef_ref):
    relative = relative_ref[...]
    octant = relative & 7
    keep = (1 - leaf_ref[...]).astype(jnp.float32)
    row = lax.broadcasted_iota(jnp.int32, (BOX_DEV, SLOTS), 0)
    selector = jnp.where(row == relative >> 3, 1.0, 0.0).astype(jnp.bfloat16)
    for block in range(1, 8):
        own = (wavelet_ref[0, block - 1].astype(jnp.float32) * keep).astype(jnp.bfloat16)
        wide_ref[block, 728:TALL] = jnp.zeros((TALL - 728, SLOTS), jnp.float32)
        wide_ref[block, 0:729] = dot(own, selector)
    line_coefficients(octant, line_ref, coef_ref)
    planes_of_blocks(wavelet_window(wide_ref), plane_ref, octant, chosen_ref)
    for p in range(9):
        out_ref[p] = line_sum(p, 18, coef_ref, chosen_ref, None)


def wavelet_window(wide_ref):
    def window(block, i):
        if block == 0:
            return jnp.zeros((WINDOW, wide_ref.shape[2]), jnp.bfloat16)
        return wide_ref[block, 81 * i : 81 * i + WINDOW].astype(jnp.bfloat16)

    return window


def spill_wavelet_kernel(halo_ref, twice_ref, plane_ref, line_ref, own_ref, after_ref, out_ref, wide_ref, chosen_ref, coef_ref, double_ref):
    lane = lax.broadcasted_iota(jnp.int32, (1, LANES), 1)
    left = lane < QUARTER
    for part in range(SLOTS // QUARTER):
        lanes = slice(LANES * (part // 2), LANES * (part // 2 + 1))
        relative = twice_ref[part : part + 1]

        @pl.when(jnp.min(relative) < 0)
        def _():
            octant = relative & 7
            parent = (relative >> 3) + SPILL
            row = lax.broadcasted_iota(jnp.int32, (LANES, LANES), 0)
            selectors = []
            for group in range(4):
                wanted = jnp.where((parent >= 0) & (parent < SPILL), parent + SPILL * group, -1)
                selectors.append(jnp.where(row == wanted, 1.0, 0.0).astype(jnp.bfloat16))
            for block in range(1, 8):
                wide_ref[block, 736:TALL] = jnp.zeros((TALL - 736, LANES), jnp.float32)
            for block, first, rows, group, place in wavelet_segments():
                wide_ref[block, first : first + rows] = dot(halo_ref[place : place + rows], selectors[group])
            line_coefficients(octant, line_ref, coef_ref)
            both = jnp.concatenate([octant, octant], axis=1)
            for j in range(5):
                even, odd = 2 * j, min(2 * j + 1, 8)

                def window(block):
                    if block == 0:
                        return jnp.zeros((WINDOW, LANES), jnp.bfloat16)
                    rows = [wide_ref[block, 81 * i : 81 * i + WINDOW] for i in (even, odd)]
                    return jnp.where(left, rows[0], rows[1]).astype(jnp.bfloat16)

                halves = [jnp.concatenate([window(4 * a + k) for k in range(4)], axis=0) for a in range(2)]
                data = jnp.concatenate(halves, axis=1)
                chosen = choose_plane(dot(plane_ref[...], jnp.concatenate([data, data], axis=0)), both)
                for a in range(2):
                    chosen_ref[5 * a + j] = chosen[:, LANES * a : LANES * (a + 1)]
                    rows = [coef_ref[81 * a + 9 * i : 81 * a + 9 * i + 9] for i in (even, odd)]
                    right = rows[1] if odd > even else jnp.zeros((9, LANES), jnp.float32)
                    double_ref[9 * (5 * a + j) : 9 * (5 * a + j) + 9] = jnp.where(left, rows[0], right)
            mine = left if part % 2 == 0 else jnp.logical_not(left)
            for p in range(9):
                total = line_sum(p, 10, double_ref, chosen_ref, None)
                total = total + pltpu.roll(total, QUARTER, 1)
                out_ref[p, :, lanes] += jnp.where(mine, total, 0.0)


def encode(values, code_ref, targets, largest_ref, scale_ref, power_ref):
    row = lax.broadcasted_iota(jnp.int32, (CHUNK, SLOTS), 0)
    for index, value in enumerate(values):
        largest_ref[index : index + 1] = jnp.max(jnp.where(row < HELD, value(), 0.0), axis=0, keepdims=True)
    largest = largest_ref[...]
    scale = jnp.full(largest.shape, 2.0**-16, jnp.float32)
    power = jnp.zeros(largest.shape, jnp.int32)
    for step in STEPS:
        longer = scale * 2.0**step
        fits = largest * longer < 32766.0
        scale = jnp.where(fits, longer, scale)
        power = jnp.where(fits, power + step, power)
    scale_ref[...] = scale
    power_ref[...] = power
    for index, value in enumerate(values):
        code = jnp.round(value() * scale_ref[index : index + 1]).astype(jnp.int32)
        code = jnp.where(row < HELD, code, power_ref[index : index + 1]).astype(jnp.int16)
        for target in targets(index):
            code_ref[target] = code


def decode_scales(code_ref, power_ref):
    for index in range(code_ref.shape[0]):
        tail = code_ref[index, CHUNK - 16 : CHUNK].astype(jnp.int32)
        power_ref[index : index + 1] = tail[15:16]
    power = power_ref[...]
    scale = jnp.full(power.shape, 2.0**16, jnp.float32)
    for step in STEPS:
        taken = power >= step
        scale = jnp.where(taken, scale * 2.0**-step, scale)
        power = jnp.where(taken, power - step, power)
    return scale


def density_kernel(pair_ref, halo_ref, relative_ref, count_ref, plane_ref, line_ref, before_ref, core_ref, dense_ref, other_ref, gathered_ref, chosen_ref, coef_ref):
    relative = relative_ref[...]
    octant = relative & 7
    selectors = parent_selectors(relative)
    spilled = jnp.concatenate([halo_ref[0], halo_ref[1]], axis=0)
    for k in range(4):
        rows = slice(192 * k, 192 * (k + 1))
        own = jnp.concatenate([pair_ref[0, rows], pair_ref[1, rows]], axis=0)
        both = dot(jnp.concatenate([own, spilled], axis=1), selectors[k]).astype(jnp.bfloat16)
        gathered_ref[0, rows] = both[0:192]
        gathered_ref[1, rows] = both[192:384]
    line_coefficients(octant, line_ref, coef_ref)
    for i in range(9):
        rows = slice(80 * i, 80 * i + WINDOW)
        high = gathered_ref[0, rows]
        planes = dot(plane_ref[i], jnp.concatenate([high, gathered_ref[1, rows], high], axis=0))
        chosen_ref[i] = choose_plane(planes, octant)
    slot = lax.broadcasted_iota(jnp.int32, (1, SLOTS), 1)
    factor = jnp.where(slot < count_ref[0, 0], 2.0, 0.0)
    dense_ref[728:744] = jnp.zeros((16, SLOTS), jnp.float32)
    for p in range(9):
        value = line_sum(p, 9, coef_ref, chosen_ref, before_ref[p])
        dense_ref[81 * p : 81 * p + PLANE] = value * value * factor
    other_ref[...] = dense_ref[half_rows(1 - core_ref[0, 0])]


def half_rows(core):
    return pl.ds(pl.multiple_of(core * HALF_ROWS, 8), HALF_ROWS)


def pair_kernel(core_ref, dense_ref, got_ref, out_ref, total_ref, largest_ref, scale_ref, shared_ref):
    total_ref[HALF_ROWS : HALF_ROWS + 8] = jnp.zeros((8, SLOTS), jnp.float32)
    total_ref[0:HALF_ROWS] = dense_ref[half_rows(core_ref[0, 0])] + got_ref[...]
    chunks = [lambda c=c: total_ref[HELD * c : HELD * c + CHUNK] for c in range(CHUNKS // 2)]
    encode(chunks, out_ref, lambda index: (index,), largest_ref, scale_ref, shared_ref)


def add_kernel(code_ref, out_ref, power_ref, inverse_ref, total_ref, largest_ref, scale_ref, shared_ref):
    inverse_ref[...] = decode_scales(code_ref, power_ref)
    total = None
    for index in range(CHUNKS // 2):
        term = code_ref[index].astype(jnp.int32).astype(jnp.float32) * inverse_ref[index : index + 1]
        total = term if total is None else total + term
    total_ref[...] = total
    encode([lambda: total_ref[...]], out_ref, lambda index: range(CHUNKS // 2), largest_ref, scale_ref, shared_ref)


def finish_kernel(code_ref, out_ref, power_ref, inverse_ref):
    inverse_ref[...] = decode_scales(code_ref, power_ref)
    for index in range(CHUNKS):
        rows = min(HELD, 729 - HELD * index)
        value = code_ref[index].astype(jnp.int32).astype(jnp.float32) * inverse_ref[index : index + 1]
        out_ref[HELD * index : HELD * index + rows] = value[0:rows]


def call(kernel, outs, scratch, *operands, scalar=(), apart=(), reuse={}):
    spaces = [pltpu.VMEM] * len(operands)
    for index in scalar:
        spaces[index] = pltpu.SMEM
    for index in apart:
        spaces[index] = pl.ANY
    return pl.pallas_call(
        kernel,
        out_shape=outs,
        in_specs=[pl.BlockSpec(memory_space=space) for space in spaces],
        out_specs=jax.tree.map(lambda out: pl.BlockSpec(memory_space=pltpu.VMEM), outs),
        scratch_shapes=[pltpu.VMEM(shape, kind) for shape, kind in scratch],
        input_output_aliases=reuse,
        compiler_params=pltpu.CompilerParams(vmem_limit_bytes=VMEM_BYTES),
    )(*operands)


def struct(shape, kind):
    return jax.ShapeDtypeStruct(shape, kind)


def pack_coarse(coarse):
    return call(
        pack_coarse_kernel, struct((PART, LANES), jnp.bfloat16), [((PART, LANES), jnp.float32)], coarse
    )


def pack_wavelets(wavelets, leaf_flags, after):
    return call(
        pack_wavelets_kernel,
        struct((SPILL_ROWS, LANES), jnp.bfloat16),
        [((SPILL_ROWS, LANES), jnp.float32)],
        wavelets, leaf_flags, after, apart=(2,),
    )


def level1(coarse, halo, relative1, table, after):
    return call(
        level1_kernel,
        [struct((2, 768, BOX_DEV), jnp.bfloat16), struct((2, 192, LANES), jnp.bfloat16)],
        [
            ((8 * TALL, BOX_DEV), jnp.float32),
            ((18, PLANE, BOX_DEV), jnp.float32),
            ((168, BOX_DEV), jnp.float32),
            ((768, BOX_DEV), jnp.float32),
        ],
        coarse, halo, relative1, table["plane1"], table["line1"], after, apart=(5,),
    )


def own_wavelets(wavelets, leaf_flags, relative2, table, after):
    return call(
        own_wavelet_kernel,
        struct((9, PLANE, SLOTS), jnp.float32),
        [((8, TALL, SLOTS), jnp.float32), ((18, PLANE, SLOTS), jnp.float32), ((168, SLOTS), jnp.float32)],
        wavelets, leaf_flags, relative2, table["plane2"], table["line2"], after, apart=(5,),
    )


def spill_wavelets(halo, relative2, table, own, after):
    quarters = relative2.reshape(SLOTS // QUARTER, QUARTER)
    return call(
        spill_wavelet_kernel,
        struct((9, PLANE, SLOTS), jnp.float32),
        [
            ((8, TALL, LANES), jnp.float32),
            ((10, PLANE, LANES), jnp.float32),
            ((168, LANES), jnp.float32),
            ((96, LANES), jnp.float32),
        ],
        halo, jnp.concatenate([quarters, quarters], axis=1), table["plane2"], table["line2"], own, after, apart=(5,), reuse={4: 0},
    )


def density_rows(pair, halo, relative2, counts, table, before, core):
    return call(
        density_kernel,
        [struct((744, SLOTS), jnp.float32), struct((HALF_ROWS, SLOTS), jnp.float32)],
        [
            ((2, 768, SLOTS), jnp.bfloat16),
            ((9, PLANE, SLOTS), jnp.float32),
            ((168, SLOTS), jnp.float32),
        ],
        pair, halo, relative2, counts, table["plane3"], table["line2"], before, core, scalar=(3, 7),
    )


def add_pair(core, dense, got):
    half = CHUNKS // 2
    return call(
        pair_kernel,
        struct((half, CHUNK, SLOTS), jnp.int16),
        [
            ((HALF_ROWS + 8, SLOTS), jnp.float32),
            ((half, SLOTS), jnp.float32),
            ((half, SLOTS), jnp.float32),
            ((half, SLOTS), jnp.int32),
        ],
        core, dense, got, scalar=(0,),
    )


def add_codes(codes):
    return call(
        add_kernel,
        struct((CHUNKS // 2, CHUNK, SLOTS), jnp.int16),
        [
            ((CHUNKS // 2, SLOTS), jnp.int32),
            ((CHUNKS // 2, SLOTS), jnp.float32),
            ((CHUNK, SLOTS), jnp.float32),
            ((1, SLOTS), jnp.float32),
            ((1, SLOTS), jnp.float32),
            ((1, SLOTS), jnp.int32),
        ],
        codes,
    )


def finish(codes):
    return call(
        finish_kernel,
        struct((729, SLOTS), jnp.float32),
        [((CHUNKS, SLOTS), jnp.int32), ((CHUNKS, SLOTS), jnp.float32)],
        codes,
    )


def shards(table, coarse, wavelets, leaf_flags, child_key1, child_key2, counts):
    position = lax.axis_index("box")
    relative1 = (child_key1 - position * (8 * BOX_DEV)).reshape(1, BOX_DEV)
    relative2 = (child_key2 - position * (8 * BOX_DEV)).reshape(1, SLOTS)
    coarse = coarse[0].transpose(1, 0, 2).reshape(ROWS, BOX_DEV)
    packed = pack_coarse(coarse)
    coarse_halo = shifted_2(packed, "box", 1)
    packed = pack_wavelets(wavelets, leaf_flags, packed)
    wavelet_halo = shifted_2(packed, "box", 1)
    own = own_wavelets(wavelets, leaf_flags, relative2, table, packed)
    pair, spill = level1(coarse, coarse_halo, relative1, table, own)
    pair_halo = shifted_2(spill, "box", 1)
    before = spill_wavelets(wavelet_halo, relative2, table, own, spill)
    core = lax.axis_index("core").reshape(1, 1)
    dense, other = density_rows(pair, pair_halo, relative2, counts.reshape(1, 1), table, before, core)
    codes = add_pair(core, dense, lax.ppermute(other, "core", [(0, 1), (1, 0)]))
    codes = lax.all_to_all(codes, "z", 0, 0, tiled=True)
    codes = lax.all_to_all(add_codes(codes), "z", 0, 0, tiled=True)
    return finish(lax.all_gather(codes, "core").reshape(CHUNKS, CHUNK, SLOTS))


def solution(mesh):
    orbitals, boxes = mesh.devices.shape
    mesh = Mesh(mesh.devices.reshape(orbitals // 2, 2, boxes), ("z", "core", "box"))
    orb = ("z", "core")
    in_specs = (P(orb, None, None, "box"), P(orb, None, None, "box"), P(orb, "box"), P("box"), P("box"), P("box"))
    out_specs = P(None, "box")
    table = {name: jnp.asarray(value) for name, value in tables().items()}
    local = functools.partial(shards, table)
    return jax.shard_map(local, mesh=mesh, in_specs=in_specs, out_specs=out_specs, check_vma=False)
```
